32 devices in a mesh: groups: 2 (over x), blk: 8 (over z, y), dp: 2 (over core).
Axes of the slice: x: 2, y: 2, z: 4, core: 2. Of those that a mesh axis runs over, the one named last changes fastest.
Arguments:
- tokens: bfloat16 [4096, 16384], P(('groups', 'blk', 'dp')), parts along dimension 0, may hold values from -6 to 6
- gain: bfloat16 [16384], replicated, may hold values from 0.29882812 to 3
- w_query: bfloat16 [16384, 1024], P('blk', 'dp')
- w_kv: bfloat16 [16384, 256], P('blk', 'dp')
- lengths: int32 [32], P('groups'), parts along dimension 0, may hold values from 1 to 1024, 2048 in all
- overlong: int32 [32], P('groups'), parts along dimension 0, may hold values 0 or 1
- assign: int32 [32], P('groups'), parts along dimension 0, may hold values from 0 to 15, as said below
Outputs:
- attended: bfloat16 [4096, 1024], P(('groups', 'blk', 'dp')), parts along dimension 0
The draws below stay inside these ranges and needn't reach their ends.
There are 2 independent parts, one for each index of `groups`. The reference program is written for one: setup_inputs(seed, part) draws one part's arguments, and reference() takes and returns one part's arrays. A program takes and returns all parts, laid end to end along the dimension named above; an argument that names none is the same for every part. Nothing has to cross between parts.
Inputs may be any that keep to these rules, and one draw needn't show every extreme that they name: `assign`: each aligned run of 2 entries holds the numbers of the row blocks of that same run, each once.
All inputs are finite; a program needn't handle non-finite values.
Results may differ from the reference program's by a relative error of at most 0.0024.
The reference program's roundings to bfloat16 on the way (of `normed`, `query` and `heads_out`) count: a program that leaves them out, or rounds other values in their place, can miss the bound.
Values may be sent and summed in bfloat16 or wider, within the bound.
No kernel may reach another device: no remote copies, remote signals or barrier semaphores. Data moves between devices by JAX's collectives and lax.ppermute only.
A program may use at most 128 MiB of HBM per device.

```python
import math
import jax
import jax.numpy as jnp
import numpy as np
from jax import lax

D = 16384
HEAD = 128
QH = 8
BLOCK = 128
TOK_DEV = 128
ROLLOUTS = 16
TOKENS = 2048
MAXLEN = 1024
BLOCKS = 16


def shared_keys(key):
    return jax.random.normal(jax.random.fold_in(key, 77), (D, HEAD), jnp.float32) * D ** (-0.5)


def draw_w_kv(key, part):
    key_cols = shared_keys(key)
    key = jax.random.fold_in(key, 13)
    values = jax.random.normal(key, (D, HEAD), jnp.float32) * D ** (-0.5)
    return jnp.concatenate([key_cols, values], axis=1).astype(jnp.bfloat16)


def draw_w_query(key, part):
    key = jax.random.fold_in(key, 11)
    matrix = jax.random.normal(key, (D, QH, HEAD), jnp.float32) * D ** (-0.5)
    return matrix.reshape(D, QH * HEAD).astype(jnp.bfloat16)


def draw_assign(key, part):
    key = jax.random.fold_in(key, 5)
    run_len = 2 * TOK_DEV // BLOCK
    runs = BLOCKS // run_len
    keys = jax.random.split(key, runs)
    orders = jax.vmap(lambda single: jax.random.permutation(single, run_len))(keys)
    firsts = (jnp.arange(runs, dtype=jnp.int32) * run_len)[:, None]
    return (orders.astype(jnp.int32) + firsts).reshape(-1).astype(jnp.int32)


def plant(drawn, own_key, low, high):
    dims = drawn.shape
    place = [jax.random.randint(jax.random.fold_in(own_key, axis), (), 0, dims[axis]) for axis in range(len(dims))]
    drawn = drawn.at[tuple(place)].set(low)
    longest = dims.index(max(dims))
    place[longest] = (place[longest] + 1) % dims[longest]
    return drawn.at[tuple(place)].set(high)


def levels(rng, extent, cuts, low, top_value):
    loudness, own = 1.0, jax.random.fold_in(rng, 6)
    for dim, blocks in cuts:
        heights = jnp.exp(jax.random.uniform(jax.random.fold_in(own, dim), (blocks,), jnp.float32, low / len(cuts), top_value / len(cuts)))
        loudness = loudness * jnp.repeat(heights, extent[dim] // blocks).reshape([-1 if axis == dim else 1 for axis in range(len(extent))])
    return loudness


def profile(number_of, total, limit, lean):
    weights = [(1 << 20) // math.isqrt(rank ** lean) + 1 for rank in range(2, number_of + 1)]
    rest, holding = total - limit - (number_of - 1), [1] * (number_of - 1)
    while rest > 0:
        free = [i for i in range(number_of - 1) if holding[i] < limit]
        mass, left = sum([weights[i] for i in free]), rest
        for i in free:
            extra = min(limit - holding[i], max(1, left * weights[i] // mass), rest)
            holding[i] = holding[i] + extra
            rest = rest - extra
    return np.array([limit] + holding)


def uneven(key, count, total, most, skew):
    if count == 2:
        one = jax.random.randint(key, (), max(1, total - most), min(most, total - 1) + 1)
        return jnp.stack([one, total - one])
    tallies = jnp.asarray(profile(count, total, most, skew), jnp.int32)
    twos = (count - 1) // 2
    source_of, sink = tallies[1:1 + 2 * twos:2], tallies[2:2 + 2 * twos:2]
    room = jnp.minimum(source_of - 1, most - sink)
    shifted = jax.random.randint(jax.random.fold_in(key, 1), (twos,), 0, 1 << 20) % (room + 1)
    tallies = tallies.at[1:1 + 2 * twos:2].set(source_of - shifted).at[2:2 + 2 * twos:2].set(sink + shifted)
    return tallies[jax.random.permutation(jax.random.fold_in(key, 2), count)]


def scatter_about(rng, shape, deviation, bound, shards=(), kind=jnp.bfloat16):
    array = jax.random.normal(rng, shape, jnp.float32) * deviation
    if len(shards) > 0:
        array = levels(rng, shape, shards, -0.22, 0.18) * array
    return jnp.clip(array, min=-bound, max=bound).astype(kind)


def setup_inputs(seed: int = 0, part: int = 0) -> dict:
    key_of = jax.random.split(jax.random.key(seed), 8)
    part_splits = jax.random.split(jax.random.fold_in(key_of[7], part), 8)
    return {
        "tokens": scatter_about(part_splits[0], (TOKENS, D), 1.0, 6.0, ((0, 16),)),
        "gain": jnp.clip(jnp.exp(jax.random.uniform(key_of[1], (D,), jnp.float32, math.log(0.29882812), math.log(3.0))), 0.29882812, 3.0).astype(jnp.bfloat16),
        "w_query": draw_w_query(jax.random.fold_in(key_of[7], 71), part),
        "w_kv": draw_w_kv(jax.random.fold_in(key_of[7], 71), part),
        "lengths": uneven(part_splits[4], ROLLOUTS, TOKENS, MAXLEN, 2).astype(jnp.int32),
        "overlong": plant((jax.random.randint(part_splits[5], (ROLLOUTS,), 0, 4) < 1).astype(jnp.int32), jax.random.fold_in(part_splits[5], 1), 0, 1),
        "assign": draw_assign(jax.random.fold_in(jax.random.fold_in(key_of[7], part), 71), part),
    }


def rollout_info(positions, lengths, overlong):
    ends = jnp.cumsum(lengths).astype(jnp.int32)
    starts = ends - lengths
    which = lax.optimization_barrier(jnp.sum((ends[None, :] <= positions[:, None]).astype(jnp.int32), axis=1))
    match = jnp.arange(lengths.shape[0], dtype=jnp.int32)[None, :] == which[:, None]
    offset = positions - lax.optimization_barrier(jnp.sum(jnp.where(match, starts[None, :], 0), axis=1))
    masked = lax.optimization_barrier(jnp.sum(jnp.where(match, overlong[None, :], 0), axis=1))
    return (which.astype(jnp.int32), offset.astype(jnp.int32), masked.astype(jnp.int32))

def rotate(vectors, offset):
    half = vectors.shape[-1] // 2
    freqs = jnp.power(jnp.float32(500000.0), -jnp.arange(half, dtype=jnp.float32) * 2.0 / vectors.shape[-1])
    angle = offset.astype(jnp.float32)[:, None] * freqs[None, :]
    cosine = jnp.cos(angle)[:, None, :]
    sine = jnp.sin(angle)[:, None, :]
    first = vectors[..., :half]
    second = vectors[..., half:]
    return jnp.concatenate([first * cosine - second * sine, second * cosine + first * sine], axis=-1)

def normalize(tokens, gain):
    widened = tokens.astype(jnp.float32)
    factor = lax.rsqrt(lax.optimization_barrier(jnp.mean(widened * widened, axis=1, keepdims=True)) + 1e-05)
    return (widened * factor * gain.astype(jnp.float32)[None, :]).astype(jnp.bfloat16)

def reference(tokens, gain, w_query, w_kv, lengths, overlong, assign):
    positions = jnp.arange(TOKENS, dtype=jnp.int32)
    which, offset, masked = rollout_info(positions, lengths, overlong)
    normed = normalize(tokens, gain)
    proj_query = jnp.dot(normed, w_query, preferred_element_type=jnp.float32)
    proj_kv = jnp.dot(normed, w_kv, preferred_element_type=jnp.float32)
    query = rotate(proj_query.reshape(TOKENS, QH, HEAD), offset).astype(jnp.bfloat16)
    key_all = rotate(proj_kv[:, :HEAD].reshape(TOKENS, 1, HEAD), offset).reshape(TOKENS, HEAD).astype(jnp.bfloat16)
    value_all = proj_kv[:, HEAD:].astype(jnp.bfloat16)
    query_blocks = query.reshape(BLOCKS, BLOCK * QH, HEAD)
    which_blocks = jnp.repeat(which, QH).reshape(BLOCKS, BLOCK * QH)
    place_blocks = jnp.repeat(positions, QH).reshape(BLOCKS, BLOCK * QH)

    def attend(inputs):
        query_rows, which_rows, place_rows = inputs
        scores = lax.dot_general(query_rows, key_all, (((1,), (1,)), ((), ())), preferred_element_type=jnp.float32) * HEAD ** (-0.5)
        valid = (which_rows[:, None] == which[None, :]) & (positions[None, :] <= place_rows[:, None])
        largest = lax.optimization_barrier(jnp.max(jnp.where(valid, scores, -1e+30), axis=1, keepdims=True))
        weights = jnp.where(valid, jnp.exp(scores - largest), 0.0)
        total = lax.optimization_barrier(jnp.sum(weights, axis=1, keepdims=True))
        summed = jnp.dot(weights.astype(jnp.bfloat16), value_all, preferred_element_type=jnp.float32)
        return summed / total
    heads = lax.map(attend, (query_blocks, which_blocks, place_blocks)).reshape(TOKENS, QH * HEAD)
    heads_out = jnp.where(masked[:, None] == 1, 0.0, heads).astype(jnp.bfloat16)
    return heads_out.reshape(BLOCKS, BLOCK * QH * HEAD)[assign].reshape(TOKENS, QH * HEAD)
```

```python
import functools

import jax
import jax.numpy as jnp
from jax import lax
from jax.sharding import Mesh
from jax.sharding import PartitionSpec as P

HEAD = 128
BLOCK = 128
CHUNK_HEADS = (2, 1, 1)


def rollout_info(positions, lengths, overlong):
    ends = jnp.cumsum(lengths)
    starts = ends - lengths
    which = jnp.sum((ends[None, :] <= positions[:, None]).astype(jnp.int32), axis=1)
    match = jnp.arange(lengths.shape[0], dtype=jnp.int32)[None, :] == which[:, None]
    offset = positions - jnp.sum(jnp.where(match, starts[None, :], 0), axis=1)
    masked = jnp.sum(jnp.where(match, overlong[None, :], 0), axis=1)
    return (which, offset, masked)


def angles(offset):
    half = HEAD // 2
    freqs = jnp.power(
        jnp.float32(500000.0), -jnp.arange(half, dtype=jnp.float32) * 2.0 / HEAD
    )
    angle = offset.astype(jnp.float32)[:, None] * freqs[None, :]
    return jnp.cos(angle), jnp.sin(angle)


def rotate(vectors, cosine, sine):
    half = HEAD // 2
    first = vectors[:, :half]
    second = vectors[:, half:]
    return jnp.concatenate(
        [first * cosine - second * sine, second * cosine + first * sine], axis=-1
    )


def shift_square(block, dx, dy, groups, ys):
    route = [
        (x * ys + y, (x + dx) % groups * ys + (y + dy) % ys)
        for x in range(groups)
        for y in range(ys)
    ]
    return lax.ppermute(block, ("groups", "y"), route)


def swap_core(block):
    return lax.ppermute(block, "dp", [(0, 1), (1, 0)])


def gather_line(block, zs):
    z = lax.axis_index("z")
    down, up = [block], [block]
    for step in range(1, zs):
        down.append(lax.ppermute(down[-1], "z", [(i, i - 1) for i in range(1, zs - step + 1)]))
        up.append(lax.ppermute(up[-1], "z", [(i, i + 1) for i in range(step - 1, zs - 1)]))
    return [block] + [jnp.where(z >= s, up[s], down[zs - s]) for s in range(1, zs)]


def on_device(groups, zs, ys, tokens, gain, w_query, w_kv, lengths, overlong, assign):
    count = tokens.shape[0]
    pair = 2 * count
    x, z, y, side = (lax.axis_index(name) for name in ("groups", "z", "y", "dp"))
    blk = z * ys + y
    part_rows = w_query.shape[0] // groups
    heads_here = w_query.shape[1] // HEAD
    offsets = [(dx, dy) for dx in range(groups) for dy in range(ys)]

    mine_q = lax.dynamic_slice_in_dim(w_query, x * part_rows, part_rows, 0)
    mine_kv = lax.dynamic_slice_in_dim(w_kv, x * part_rows, part_rows, 0)
    chunks = [mine_kv]
    at = 0
    for heads in CHUNK_HEADS:
        chunks.append(mine_q[:, at * HEAD : (at + heads) * HEAD])
        at += heads
    weights = [jnp.concatenate(gather_line(chunk, zs), axis=0) for chunk in chunks]

    factor = lax.rsqrt(
        jnp.mean(jnp.square(tokens.astype(jnp.float32)), axis=1, keepdims=True) + 1e-05
    )

    def columns_of(dx, dy):
        pieces = []
        for s in range(zs):
            start = (((z - s) % zs * ys + (y + dy) % ys) * groups + (x + dx) % groups) * part_rows
            part = lax.dynamic_slice_in_dim(tokens, start, part_rows, 1).astype(jnp.float32)
            scale = lax.dynamic_slice_in_dim(gain, start, part_rows, 0).astype(jnp.float32)
            pieces.append((part * factor * scale[None, :]).astype(jnp.bfloat16))
        return jnp.concatenate(pieces, axis=1)

    pieces = [shift_square(columns_of(dx, dy), dx, dy, groups, ys) if dx or dy else columns_of(0, 0) for dx, dy in offsets]
    others = [swap_core(piece) for piece in pieces]
    rows_of = [
        jnp.where(side == 0, jnp.concatenate([a, b], axis=0), jnp.concatenate([b, a], axis=0))
        for a, b in zip(pieces, others)
    ]

    def project(weight):
        total = None
        for (dx, dy), rows in zip(offsets, rows_of):
            partial = jnp.dot(rows, weight, preferred_element_type=jnp.float32)
            if dx or dy:
                partial = shift_square(partial, -dx, -dy, groups, ys)
            total = partial if total is None else total + partial
        return total

    pair_base = blk * pair
    pair_rows = pair_base + jnp.arange(pair, dtype=jnp.int32)
    which, offset, masked = rollout_info(pair_rows, lengths, overlong)
    cosine, sine = angles(offset)

    proj = project(weights[0])
    kept = jnp.where(side == 0, rotate(proj, cosine, sine), proj).astype(jnp.bfloat16)
    along = [kept] + [
        lax.ppermute(kept, "z", [(i, (i + s) % zs) for i in range(zs)]) for s in range(1, zs)
    ]
    along = jnp.concatenate(along, axis=0)
    halves = [along] + [
        lax.ppermute(along, "y", [(i, (i + s) % ys) for i in range(ys)]) for s in range(1, ys)
    ]
    here = jnp.concatenate(halves, axis=0)
    there = swap_core(here)
    key = jnp.where(side == 0, here, there)
    value = jnp.where(side == 0, there, here)
    key_blk = jnp.stack([(z - s) % zs * ys + (y - t) % ys for t in range(ys) for s in range(zs)])
    key_place = (
        key_blk[:, None] * pair + jnp.arange(pair, dtype=jnp.int32)[None, :]
    ).reshape(-1)
    ends = jnp.cumsum(lengths)
    key_which = jnp.sum((ends[None, :] <= key_place[:, None]).astype(jnp.int32), axis=1)
    valid = (which[:, None] == key_which[None, :]) & (key_place[None, :] <= pair_rows[:, None])

    def attend(query):
        scores = lax.dot_general(
            query, key, (((1,), (1,)), ((), ())), preferred_element_type=jnp.float32
        ) * HEAD ** (-0.5)
        newest = jnp.max(jnp.where(valid, scores, -1e30), axis=1)
        weight = jnp.where(valid, jnp.exp(scores - newest[:, None]), 0.0)
        total = jnp.sum(weight, axis=1)
        summed = jnp.dot(weight.astype(jnp.bfloat16), value, preferred_element_type=jnp.float32)
        out = summed / total[:, None]
        return jnp.where(masked[:, None] == 1, 0.0, out).astype(jnp.bfloat16)

    first = pair_base // BLOCK
    slots = lax.dynamic_slice_in_dim(assign, first, 2) - first
    own_slot = lax.dynamic_index_in_dim(slots, side, keepdims=False)
    other_slot = lax.dynamic_index_in_dim(slots, 1 - side, keepdims=False)
    kept_out, got_out = [], []
    for heads, weight in zip(CHUNK_HEADS, weights[1:]):
        proj = project(weight)
        outs = []
        for head in range(heads):
            query = rotate(proj[:, head * HEAD : (head + 1) * HEAD], cosine, sine)
            outs.append(attend(query.astype(jnp.bfloat16)))
        outs = jnp.concatenate(outs, axis=1)
        kept_out.append(lax.dynamic_slice_in_dim(outs, own_slot * BLOCK, BLOCK, 0))
        got_out.append(swap_core(lax.dynamic_slice_in_dim(outs, other_slot * BLOCK, BLOCK, 0)))
    kept_out = jnp.concatenate(kept_out, axis=1)
    got_out = jnp.concatenate(got_out, axis=1)
    return jnp.where(
        side == 0,
        jnp.concatenate([kept_out, got_out], axis=1),
        jnp.concatenate([got_out, kept_out], axis=1),
    )


def solution(mesh):
    groups, blks, cores = (mesh.shape[name] for name in ("groups", "blk", "dp"))
    ys = 2
    zs = blks // ys
    fine = Mesh(mesh.devices.reshape(groups, zs, ys, cores), ("groups", "z", "y", "dp"))
    placed = (
        P(("groups", "z", "y", "dp"), None),
        P(),
        P(("z", "y"), "dp"),
        P(("z", "y"), "dp"),
        P("groups"),
        P("groups"),
        P("groups"),
    )
    return jax.shard_map(
        functools.partial(on_device, groups, zs, ys),
        mesh=fine,
        in_specs=placed,
        out_specs=P(("groups", "z", "y", "dp"), None),
        check_vma=False,
    )
```

```python
import functools

import jax
import jax.numpy as jnp
from jax import lax
from jax.experimental import pallas as pl
from jax.experimental.pallas import tpu as pltpu
from jax.sharding import Mesh
from jax.sharding import PartitionSpec as P

HEAD = 128
BLOCK = 128
CHUNK_HEADS = (1, 2, 1)
VMEM = 48 * 1024 * 1024


def rollout_info(positions, lengths, overlong):
    ends = jnp.cumsum(lengths)
    starts = ends - lengths
    which = jnp.sum((ends[None, :] <= positions[:, None]).astype(jnp.int32), axis=1)
    match = jnp.arange(lengths.shape[0], dtype=jnp.int32)[None, :] == which[:, None]
    offset = positions - jnp.sum(jnp.where(match, starts[None, :], 0), axis=1)
    masked = jnp.sum(jnp.where(match, overlong[None, :], 0), axis=1)
    return (which, offset, masked)


def rotation(offset):
    half = HEAD // 2
    freqs = jnp.power(
        jnp.float32(500000.0), -jnp.arange(half, dtype=jnp.float32) * 2.0 / HEAD
    )
    angle = offset.astype(jnp.float32)[:, None] * freqs[None, :]
    cosine, sine = jnp.cos(angle), jnp.sin(angle)
    return jnp.concatenate([cosine, cosine], axis=1), jnp.concatenate([-sine, sine], axis=1)


def shift_square(block, dx, dy, groups, ys):
    route = [
        (x * ys + y, (x + dx) % groups * ys + (y + dy) % ys)
        for x in range(groups)
        for y in range(ys)
    ]
    return lax.ppermute(block, ("groups", "y"), route)


def swap_core(block):
    return lax.ppermute(block, "dp", [(0, 1), (1, 0)])


def gather_line(block, zs):
    down, up = [block], [block]
    for step in range(1, zs):
        down.append(lax.ppermute(down[-1], "z", [(i, i - 1) for i in range(1, zs - step + 1)]))
        up.append(lax.ppermute(up[-1], "z", [(i, i + 1) for i in range(step - 1, zs - 1)]))
    return down, up


def norm_kernel(zs, ys, groups, width, place, tokens, gain, *outs):
    x, z, y = place[0], place[1], place[2]
    rows, columns = tokens.shape
    step = min(columns, 1024)
    squares = jnp.zeros((rows, step), jnp.float32)
    for at in range(0, columns, step):
        part = tokens[:, at : at + step].astype(jnp.float32)
        squares += part * part
    factor = lax.rsqrt(jnp.sum(squares, axis=1, keepdims=True) / columns + 1e-05)
    for peer, out in enumerate(outs):
        dx, dy = peer // ys, peer % ys
        for s in range(zs):
            blk = lax.rem(z + (zs - s), zs) * ys + lax.rem(y + dy, ys)
            start = pl.multiple_of((blk * groups + lax.rem(x + dx, groups)) * width, width)
            part = tokens[:, pl.ds(start, width)].astype(jnp.float32)
            scale = gain[:, pl.ds(start, width)]
            out[:, s * width : (s + 1) * width] = (part * factor * scale).astype(jnp.bfloat16)


def norm_pieces(tokens, gain, place, zs, ys, groups, width):
    count, columns = tokens.shape
    rows = min(count, 32)
    peers = groups * ys
    return pl.pallas_call(
        functools.partial(norm_kernel, zs, ys, groups, width),
        grid=(count // rows,),
        in_specs=[
            pl.BlockSpec(memory_space=pltpu.SMEM),
            pl.BlockSpec((rows, columns), lambda i: (i, 0)),
            pl.BlockSpec((1, columns), lambda i: (0, 0)),
        ],
        out_specs=[pl.BlockSpec((rows, zs * width), lambda i: (i, 0))] * peers,
        out_shape=[jax.ShapeDtypeStruct((count, zs * width), jnp.bfloat16)] * peers,
        compiler_params=pltpu.CompilerParams(vmem_limit_bytes=VMEM),
        cost_estimate=pl.CostEstimate(
            flops=5 * count * columns, bytes_accessed=4 * count * columns, transcendentals=count
        ),
        name="norm",
    )(place, tokens, gain.astype(jnp.float32)[None, :])


def project_kernel(zs, peers, place, *refs):
    mine, others = refs[:peers], refs[peers : 2 * peers]
    weights = refs[2 * peers : 2 * peers + 2 * zs - 1]
    own, down, up = weights[0], weights[1:zs], weights[zs:]
    outs = refs[2 * peers + 2 * zs - 1 :]
    z, side = place[1], place[3]
    count = mine[0].shape[0]
    width = own.shape[0]
    total = None
    for s in range(zs):
        columns = slice(s * width, (s + 1) * width)
        rows = jnp.concatenate([ref[:, columns] for ref in mine + others], axis=0)
        weight = own[...] if s == 0 else jnp.where(z >= s, up[s - 1][...], down[zs - s - 1][...])
        product = jnp.dot(rows, weight, preferred_element_type=jnp.float32)
        total = product if total is None else total + product
    for peer, out in enumerate(outs):
        here = pl.multiple_of(side * count, count)
        there = pl.multiple_of((1 - side) * count, count)
        out[pl.ds(here, count), :] = total[peer * count : (peer + 1) * count]
        out[pl.ds(there, count), :] = total[(peers + peer) * count : (peers + peer + 1) * count]


def project(pieces, others, down, up, place, zs):
    peers = len(pieces)
    count = pieces[0].shape[0]
    width, columns = down[0].shape
    operands = [place, *pieces, *others, *down, *up[1:]]
    return pl.pallas_call(
        functools.partial(project_kernel, zs, peers),
        in_specs=[pl.BlockSpec(memory_space=pltpu.SMEM)]
        + [pl.BlockSpec(memory_space=pltpu.VMEM)] * (len(operands) - 1),
        out_specs=[pl.BlockSpec(memory_space=pltpu.VMEM)] * peers,
        out_shape=[jax.ShapeDtypeStruct((2 * count, columns), jnp.float32)] * peers,
        compiler_params=pltpu.CompilerParams(vmem_limit_bytes=VMEM),
        cost_estimate=pl.CostEstimate(
            flops=4 * peers * count * zs * width * columns,
            bytes_accessed=4 * peers * count * zs * width,
            transcendentals=0,
        ),
        name="project",
    )(*operands)


def attend_kernel(heads, peers, first, place, *refs):
    partials = refs[:peers]
    cosine, sine, query_info, key_info, here, there, kept, sent = refs[peers:]
    side, own_slot, other_slot = place[3], place[4], place[5]
    key = jnp.where(side == 0, here[...], there[...])
    value = jnp.where(side == 0, there[...], here[...])
    which, position, masked = query_info[:, 0:1], query_info[:, 1:2], query_info[:, 2:3]
    valid = (which == key_info[0:1, :]) & (key_info[1:2, :] <= position)
    for head in range(heads):
        columns = slice((first + head) * HEAD, (first + head + 1) * HEAD)
        proj = partials[0][:, columns]
        for other in partials[1:]:
            proj = proj + other[:, columns]
        turned = proj * cosine[...] + pltpu.roll(proj, HEAD // 2, 1) * sine[...]
        scores = lax.dot_general(
            turned.astype(jnp.bfloat16),
            key,
            (((1,), (1,)), ((), ())),
            preferred_element_type=jnp.float32,
        ) * HEAD ** (-0.5)
        largest = jnp.max(jnp.where(valid, scores, -1e30), axis=1, keepdims=True)
        weights = jnp.where(valid, jnp.exp(scores - largest), 0.0)
        total = jnp.sum(weights, axis=1, keepdims=True)
        summed = jnp.dot(weights.astype(jnp.bfloat16), value, preferred_element_type=jnp.float32)
        out = jnp.where(masked == 1, 0.0, summed / total).astype(jnp.bfloat16)
        low, high = out[:BLOCK], out[BLOCK:]
        into = slice(head * HEAD, (head + 1) * HEAD)
        kept[:, into] = jnp.where(own_slot == 0, low, high)
        sent[:, into] = jnp.where(other_slot == 0, low, high)


def attend(heads, first, partials, cosine, sine, query_info, key_info, here, there, place):
    rows, keys = cosine.shape[0], here.shape[0]
    operands = [place, *partials, cosine, sine, query_info, key_info, here, there]
    return pl.pallas_call(
        functools.partial(attend_kernel, heads, len(partials), first),
        in_specs=[pl.BlockSpec(memory_space=pltpu.SMEM)]
        + [pl.BlockSpec(memory_space=pltpu.VMEM)] * (len(operands) - 1),
        out_specs=[pl.BlockSpec(memory_space=pltpu.VMEM)] * 2,
        out_shape=[jax.ShapeDtypeStruct((BLOCK, heads * HEAD), jnp.bfloat16)] * 2,
        compiler_params=pltpu.CompilerParams(vmem_limit_bytes=VMEM),
        cost_estimate=pl.CostEstimate(
            flops=4 * heads * rows * keys * HEAD,
            bytes_accessed=4 * keys * HEAD + 20 * rows * heads * HEAD,
            transcendentals=heads * rows * keys,
        ),
        name="attend",
    )(*operands)


def on_device(groups, zs, ys, tokens, gain, w_query, w_kv, lengths, overlong, assign):
    count = tokens.shape[0]
    pair = 2 * count
    x, z, y, side = (lax.axis_index(name) for name in ("groups", "z", "y", "dp"))
    blk = z * ys + y
    width = w_query.shape[0] // groups
    peers = [(dx, dy) for dx in range(groups) for dy in range(ys)]
    pair_base = blk * pair
    block_base = pair_base // BLOCK
    slots = lax.dynamic_slice_in_dim(assign, block_base, 2) - block_base
    own_slot = lax.dynamic_index_in_dim(slots, side, keepdims=False)
    other_slot = lax.dynamic_index_in_dim(slots, 1 - side, keepdims=False)
    place = jnp.stack([x, z, y, side, own_slot, other_slot]).astype(jnp.int32)

    mine_q = lax.dynamic_slice_in_dim(w_query, x * width, width, 0)
    mine_kv = lax.dynamic_slice_in_dim(w_kv, x * width, width, 0)
    chunks, at = [], 0
    for heads in CHUNK_HEADS:
        chunk = mine_q[:, at * HEAD : (at + heads) * HEAD]
        chunks.append(jnp.concatenate([mine_kv, chunk], axis=1) if at == 0 else chunk)
        at += heads

    normed = norm_pieces(tokens, gain, place, zs, ys, groups, width)
    normed, chunks[1:] = lax.optimization_barrier((normed, chunks[1:]))
    weights = [gather_line(chunk, zs) for chunk in chunks]
    pieces = [
        shift_square(piece, dx, dy, groups, ys) if dx or dy else piece
        for (dx, dy), piece in zip(peers, normed)
    ]
    others = [swap_core(piece) for piece in pieces]

    def partial_sums(chunk):
        down, up = weights[chunk]
        sums = project(pieces, others, down, up, place, zs)
        return [
            shift_square(part, -dx, -dy, groups, ys) if dx or dy else part
            for (dx, dy), part in zip(peers, sums)
        ]

    pair_rows = pair_base + jnp.arange(pair, dtype=jnp.int32)
    which, offset, masked = rollout_info(pair_rows, lengths, overlong)
    cosine, sine = rotation(offset)
    query_info = jnp.stack([which, pair_rows, masked], axis=1)
    key_blk = jnp.stack([(z - s) % zs * ys + (y - t) % ys for t in range(ys) for s in range(zs)])
    key_place = (
        key_blk[:, None] * pair + jnp.arange(pair, dtype=jnp.int32)[None, :]
    ).reshape(-1)
    ends = jnp.cumsum(lengths)
    key_which = jnp.sum((ends[None, :] <= key_place[:, None]).astype(jnp.int32), axis=1)
    key_info = jnp.stack([key_which, key_place], axis=0)

    partials = partial_sums(0)
    proj = sum(part[:, :HEAD] for part in partials)
    turned = proj * cosine + jnp.roll(proj, HEAD // 2, axis=1) * sine
    mine = jnp.where(side == 0, turned, proj).astype(jnp.bfloat16)
    along = [mine] + [
        lax.ppermute(mine, "z", [(i, (i + s) % zs) for i in range(zs)]) for s in range(1, zs)
    ]
    along = jnp.concatenate(along, axis=0)
    here = [along] + [
        lax.ppermute(along, "y", [(i, (i + s) % ys) for i in range(ys)]) for s in range(1, ys)
    ]
    here = jnp.concatenate(here, axis=0)
    there = swap_core(here)

    kept, got = [], []
    for chunk, heads in enumerate(CHUNK_HEADS):
        if chunk:
            partials = partial_sums(chunk)
        own, other = attend(
            heads, 0 if chunk else 1, partials, cosine, sine, query_info, key_info, here, there, place
        )
        kept.append(own)
        got.append(swap_core(other))
    kept = jnp.concatenate(kept, axis=1)
    got = jnp.concatenate(got, axis=1)
    return jnp.where(
        side == 0,
        jnp.concatenate([kept, got], axis=1),
        jnp.concatenate([got, kept], axis=1),
    )


def solution(mesh):
    groups, blks, cores = (mesh.shape[name] for name in ("groups", "blk", "dp"))
    ys = 2
    zs = blks // ys
    fine = Mesh(mesh.devices.reshape(groups, zs, ys, cores), ("groups", "z", "y", "dp"))
    placed = (
        P(("groups", "z", "y", "dp"), None),
        P(),
        P(("z", "y"), "dp"),
        P(("z", "y"), "dp"),
        P("groups"),
        P("groups"),
        P("groups"),
    )
    return jax.shard_map(
        functools.partial(on_device, groups, zs, ys),
        mesh=fine,
        in_specs=placed,
        out_specs=P(("groups", "z", "y", "dp"), None),
        check_vma=False,
    )
```

```python
import functools

import jax
import jax.numpy as jnp
from jax import lax
from jax.experimental import pallas as pl
from jax.experimental.pallas import tpu as pltpu
from jax.sharding import Mesh
from jax.sharding import PartitionSpec as P

HEAD = 128
BLOCK = 128
CHUNK_HEADS = (2, 2)
MIB = 1024 * 1024
COST = pl.CostEstimate(flops=1, bytes_accessed=1, transcendentals=0)


def rollout_info(positions, lengths, overlong):
    ends = jnp.cumsum(lengths)
    starts = ends - lengths
    which = jnp.sum((ends[None, :] <= positions[:, None]).astype(jnp.int32), axis=1)
    match = jnp.arange(lengths.shape[0], dtype=jnp.int32)[None, :] == which[:, None]
    offset = positions - jnp.sum(jnp.where(match, starts[None, :], 0), axis=1)
    masked = jnp.sum(jnp.where(match, overlong[None, :], 0), axis=1)
    return (which, offset, masked)


def rotation(offset):
    half = HEAD // 2
    freqs = jnp.power(
        jnp.float32(500000.0), -jnp.arange(half, dtype=jnp.float32) * 2.0 / HEAD
    )
    angle = offset.astype(jnp.float32)[:, None] * freqs[None, :]
    cosine, sine = jnp.cos(angle), jnp.sin(angle)
    return jnp.concatenate([cosine, cosine], axis=1), jnp.concatenate([-sine, sine], axis=1)


def shift_square(block, dx, dy, groups, ys):
    route = [
        (x * ys + y, (x + dx) % groups * ys + (y + dy) % ys)
        for x in range(groups)
        for y in range(ys)
    ]
    return lax.ppermute(block, ("groups", "y"), route)


def swap_core(block):
    return lax.ppermute(block, "dp", [(0, 1), (1, 0)])


def after(block, *done):
    return lax.optimization_barrier((block, *done))[0]


def hop_down(block, step, zs):
    with jax.named_scope("hop%d_down" % step):
        return lax.ppermute(block, "z", [(i, i - 1) for i in range(1, zs - step + 1)])


def hop_up(block, step, zs):
    with jax.named_scope("hop%d_up" % step):
        return lax.ppermute(block, "z", [(i, i + 1) for i in range(step - 1, zs - 1)])


def hop_ends(block, zs):
    with jax.named_scope("hop_ends"):
        return lax.ppermute(block, "z", [(1, 0), (zs - 2, zs - 1)])


def nearest(z, place, zs):
    low = jnp.minimum(z, zs - 1 - z)
    step = (place + 1) // 2
    inner = z - step if place % 2 else z + step
    return jnp.where(place <= 2 * low, inner, jnp.where(2 * z < zs, place, zs - 1 - place))


def ways(place, zs):
    if place == 0:
        return [(None, "own", 0)]
    step = (place + 1) // 2
    inner = [(None, "up" if place % 2 else "down", step)] if place <= zs - 2 else []
    ends = [z for z in range(zs // 2) if 2 * z < place]
    return (
        inner
        + [(z, "down", place - z) for z in ends]
        + [(zs - 1 - z, "up", place - z) for z in ends]
    )


def norm_kernel(zs, ys, groups, width, tokens, gain, out):
    z = lax.axis_index("z")
    rows, columns = tokens.shape
    step = min(columns, 1024)
    squares = jnp.zeros((rows, step), jnp.float32)
    for at in range(0, columns, step):
        part = tokens[:, at : at + step].astype(jnp.float32)
        squares += part * part
    factor = lax.rsqrt(jnp.sum(squares, axis=1, keepdims=True) / columns + 1e-05)
    for s in range(zs):
        into = slice(s * width, (s + 1) * width)
        for peer in range(groups * ys):
            x, y = peer // ys, peer % ys
            blk = nearest(z, s, zs) * ys + y
            start = pl.multiple_of((blk * groups + x) * width, width)
            part = tokens[:, pl.ds(start, width)].astype(jnp.float32)
            scale = gain[:, pl.ds(start, width)]
            out[peer, :, into] = (part * factor * scale).astype(jnp.bfloat16)


def norm_pieces(tokens, gain, zs, ys, groups, width):
    count, columns = tokens.shape
    rows = min(count, 32)
    shape = (groups * ys, count, zs * width)
    return pl.pallas_call(
        functools.partial(norm_kernel, zs, ys, groups, width),
        grid=(count // rows,),
        in_specs=[
            pl.BlockSpec((rows, columns), lambda i: (i, 0)),
            pl.BlockSpec((1, columns), lambda i: (0, 0)),
        ],
        out_specs=pl.BlockSpec((shape[0], rows, shape[2]), lambda i: (0, i, 0)),
        out_shape=jax.ShapeDtypeStruct(shape, jnp.bfloat16),
        compiler_params=pltpu.CompilerParams(vmem_limit_bytes=24 * MIB),
        cost_estimate=COST,
        name="norm",
    )(tokens, gain.astype(jnp.float32)[None, :])


def peer_order(ys, groups, peers):
    x, y = lax.axis_index("groups"), lax.axis_index("y")
    return [
        lax.rem(x + (groups - peer // ys), groups) * ys + lax.rem(y + (ys - peer % ys), ys)
        for peer in range(peers)
    ]


def collect_kernel(zs, ys, groups, names, cuts, *refs):
    mine, others = refs[:2]
    weights, outs = dict(zip(names, refs[2:])), refs[2 + len(names) :]
    z = lax.axis_index("z")
    base, size = cuts[0][0], sum(size for _, size in cuts)
    peers, _, columns = mine.shape
    width = columns // zs
    index = peer_order(ys, groups, peers)
    total = None
    for place in range(zs):
        into = slice(place * width, (place + 1) * width)
        rows = jnp.concatenate([ref[i, :, into] for ref in (mine, others) for i in index], axis=0)
        weight = None
        for who, way, hops in ways(place, zs):
            if (way, hops) in weights:
                read = weights[way, hops][:, base : base + size]
                if weight is None:
                    weight = read if who is None else jnp.where(z == who, read, jnp.zeros_like(read))
                else:
                    weight = jnp.where(z == who, read, weight)
        product = jnp.dot(rows, weight, preferred_element_type=jnp.float32)
        total = product if total is None else total + product
    for (first, size), out in zip(cuts, outs):
        out[...] = total[:, first - base : first - base + size]


def collect(mine, others, pieces, cuts, zs, ys, groups):
    rows = 2 * mine.shape[0] * mine.shape[1]
    operands = [mine, others, *pieces.values()]
    return pl.pallas_call(
        functools.partial(collect_kernel, zs, ys, groups, list(pieces), cuts),
        in_specs=[pl.BlockSpec(memory_space=pltpu.VMEM)] * len(operands),
        out_specs=[pl.BlockSpec(memory_space=pltpu.VMEM)] * len(cuts),
        out_shape=[jax.ShapeDtypeStruct((rows, size), jnp.float32) for _, size in cuts],
        compiler_params=pltpu.CompilerParams(vmem_limit_bytes=40 * MIB),
        cost_estimate=COST,
        name="collect",
    )(*operands)


def finish_kernel(ys, groups, cuts, mine, others, last, sums, *outs):
    side = lax.axis_index("dp")
    peers, count = mine.shape[:2]
    index = peer_order(ys, groups, peers)
    rows = jnp.concatenate([ref[i] for ref in (mine, others) for i in index], axis=0)
    total = sums[...] + jnp.dot(rows, last[...], preferred_element_type=jnp.float32)
    here = pl.multiple_of(side * count, count)
    there = pl.multiple_of((1 - side) * count, count)
    for at, out in enumerate(outs):
        first, size = cuts[at // peers]
        peer = at % peers
        part = total[:, first : first + size]
        out[pl.ds(here, count), :] = part[peer * count : (peer + 1) * count]
        out[pl.ds(there, count), :] = part[(peers + peer) * count : (peers + peer + 1) * count]


def finish(mine, others, last, sums, cuts, ys, groups):
    peers, count, columns = mine.shape
    width = last.shape[0]
    tokens = pl.BlockSpec((peers, count, width), lambda i: (0, 0, columns // width - 1))
    sizes = [size for _, size in cuts for _ in range(peers)]
    outs = pl.pallas_call(
        functools.partial(finish_kernel, ys, groups, cuts),
        grid=(1,),
        in_specs=[
            tokens,
            tokens,
            pl.BlockSpec(last.shape, lambda i: (0, 0)),
            pl.BlockSpec(sums.shape, lambda i: (0, 0)),
        ],
        out_specs=[pl.BlockSpec((2 * count, size), lambda i: (0, 0)) for size in sizes],
        out_shape=[jax.ShapeDtypeStruct((2 * count, size), jnp.float32) for size in sizes],
        compiler_params=pltpu.CompilerParams(vmem_limit_bytes=32 * MIB),
        cost_estimate=COST,
        name="finish",
    )(mine, others, last, sums)
    return [outs[at * peers : (at + 1) * peers] for at in range(len(cuts))]


def attend_kernel(peers, window, place, *refs):
    partials = refs[:peers]
    cosine, sine, query_info, which_key, here, there, kept, sent = refs[peers:]
    side, own_slot, other_slot, first = place[0], place[1], place[2], place[3]
    rows = cosine.shape[0]
    spots = [place[4 + i] for i in range(window // rows)]
    here, there = (
        jnp.concatenate([ref[pl.ds(pl.multiple_of(at, rows), rows), :] for at in spots], axis=0)
        for ref in (here, there)
    )
    key = jnp.where(side == 0, here, there)
    value = jnp.where(side == 0, there, here)
    which, position, masked = query_info[:, 0:1], query_info[:, 1:2], query_info[:, 2:3]
    key_position = first + lax.broadcasted_iota(jnp.int32, (1, window), 1)
    valid = (which == which_key[...]) & (key_position <= position)
    proj = partials[0][...]
    for other in partials[1:]:
        proj = proj + other[...]
    turned = proj * cosine[...] + pltpu.roll(proj, HEAD // 2, 1) * sine[...]
    scores = lax.dot_general(
        turned.astype(jnp.bfloat16), key, (((1,), (1,)), ((), ())), preferred_element_type=jnp.float32
    ) * HEAD ** (-0.5)
    largest = jnp.max(jnp.where(valid, scores, -1e30), axis=1, keepdims=True)
    weights = jnp.where(valid, jnp.exp(scores - largest), 0.0)
    total = jnp.sum(weights, axis=1, keepdims=True)
    summed = jnp.dot(weights.astype(jnp.bfloat16), value, preferred_element_type=jnp.float32)
    out = jnp.where(masked == 1, 0.0, summed / total).astype(jnp.bfloat16)
    low, high = out[:BLOCK], out[BLOCK:]
    kept[...] = jnp.where(own_slot == 0, low, high)
    sent[...] = jnp.where(other_slot == 0, low, high)


def attend(partials, cosine, sine, query_info, which_key, here, there, place):
    rows, window = cosine.shape[0], which_key.shape[1]
    heads = partials[0].shape[1] // HEAD
    fixed = [cosine, sine, query_info, which_key, here, there]
    return pl.pallas_call(
        functools.partial(attend_kernel, len(partials), window),
        grid=(heads,),
        in_specs=[pl.BlockSpec(memory_space=pltpu.SMEM)]
        + [pl.BlockSpec((rows, HEAD), lambda h: (0, h))] * len(partials)
        + [pl.BlockSpec(array.shape, lambda h: (0, 0)) for array in fixed],
        out_specs=[pl.BlockSpec((BLOCK, HEAD), lambda h: (0, h))] * 2,
        out_shape=[jax.ShapeDtypeStruct((BLOCK, heads * HEAD), jnp.bfloat16)] * 2,
        compiler_params=pltpu.CompilerParams(vmem_limit_bytes=16 * MIB + 24 * rows * window),
        cost_estimate=COST,
        name="attend",
    )(place, *partials, *fixed)


def on_device(groups, zs, ys, tokens, gain, w_query, w_kv, lengths, overlong, assign):
    count = tokens.shape[0]
    pair = 2 * count
    x, z, y, side = (lax.axis_index(name) for name in ("groups", "z", "y", "dp"))
    blk = z * ys + y
    width = w_query.shape[0] // groups
    peers = [(dx, dy) for dx in range(groups) for dy in range(ys)]
    pair_base = blk * pair
    block_base = pair_base // BLOCK
    slots = lax.dynamic_slice_in_dim(assign, block_base, 2) - block_base
    own_slot = lax.dynamic_index_in_dim(slots, side, keepdims=False)
    other_slot = lax.dynamic_index_in_dim(slots, 1 - side, keepdims=False)
    tokens_all = zs * ys * pair
    window = min(tokens_all // 2 + pair, tokens_all)
    first_key = jnp.maximum(pair_base - tokens_all // 2, 0)
    key_blk = first_key // pair + jnp.arange(window // pair, dtype=jnp.int32)
    spot = (blk % ys + ys - key_blk % ys) % ys * zs + (z + zs - key_blk // ys) % zs
    place = jnp.concatenate(
        [jnp.stack([side, own_slot, other_slot, first_key]).astype(jnp.int32), spot * pair]
    )

    own = jnp.concatenate(
        [
            lax.dynamic_slice_in_dim(w_kv, x * width, width, 0),
            lax.dynamic_slice_in_dim(w_query, x * width, width, 0),
        ],
        axis=1,
    )
    normed = norm_pieces(tokens, gain, zs, ys, groups, width)
    mine = lax.all_to_all(normed, ("groups", "y"), 0, 0, tiled=True)
    pieces = {("own", 0): own}
    came = [after(own, normed), after(own, normed)]
    for step in range(1, zs - 1):
        came = [hop_down(came[0], step, zs), hop_up(came[1], step, zs)]
        pieces["down", step], pieces["up", step] = came
    done = (mine, *came)
    others = swap_core(after(mine, *done))
    came = [after(came[0], *done), after(came[1], *done)]
    cuts, first = [(0, HEAD)], HEAD
    for heads in CHUNK_HEADS:
        cuts.append((first, heads * HEAD))
        first += heads * HEAD
    last = [
        hop_ends(jnp.where(z == 1, came[0][:, a : a + n], came[1][:, a : a + n]), zs)
        for a, n in cuts
    ]
    sums = [
        *collect(mine, others, pieces, cuts[:1], zs, ys, groups),
        *collect(mine, others, pieces, cuts[1:], zs, ys, groups),
    ]

    def partial_sums(part):
        inner = [(0, cuts[part][1])]
        (parts,) = finish(mine, others, last[part], sums[part], inner, ys, groups)
        return [
            shift_square(part_of, -dx, -dy, groups, ys) if dx or dy else part_of
            for (dx, dy), part_of in zip(peers, parts)
        ]

    pair_rows = pair_base + jnp.arange(pair, dtype=jnp.int32)
    which, offset, masked = rollout_info(pair_rows, lengths, overlong)
    cosine, sine = rotation(offset)
    query_info = jnp.stack([which, pair_rows, masked], axis=1)
    key_place = first_key + jnp.arange(window, dtype=jnp.int32)
    ends = jnp.cumsum(lengths)
    which_key = jnp.sum((ends[:, None] <= key_place[None, :]).astype(jnp.int32), axis=0)[None, :]

    proj = sum(partial_sums(0))
    turned = proj * cosine + jnp.roll(proj, HEAD // 2, axis=1) * sine
    kept_kv = jnp.where(side == 0, turned, proj).astype(jnp.bfloat16)
    kept_kv, last[1] = lax.optimization_barrier((kept_kv, last[1]))
    along = [
        lax.ppermute(kept_kv, "z", [(i, (i + n) % zs) for i in range(zs)]) for n in range(1, zs)
    ]
    along, last[2] = lax.optimization_barrier((along, last[2]))
    along = jnp.concatenate([kept_kv, *along], axis=0)
    beside = lax.ppermute(along, "y", [(i, (i + 1) % ys) for i in range(ys)])
    here = jnp.concatenate([along, beside], axis=0)
    there = swap_core(here)

    kept, got = [], []
    for part in range(1, len(cuts)):
        partials = partial_sums(part)
        owned, other = attend(partials, cosine, sine, query_info, which_key, here, there, place)
        kept.append(owned)
        got.append(swap_core(other))
    kept = jnp.concatenate(kept, axis=1)
    got = jnp.concatenate(got, axis=1)
    return jnp.where(
        side == 0,
        jnp.concatenate([kept, got], axis=1),
        jnp.concatenate([got, kept], axis=1),
    )


def solution(mesh):
    groups, blks, cores = (mesh.shape[name] for name in ("groups", "blk", "dp"))
    ys = 2
    zs = blks // ys
    fine = Mesh(mesh.devices.reshape(groups, zs, ys, cores), ("groups", "z", "y", "dp"))
    placed = (
        P(("groups", "z", "y", "dp"), None),
        P(),
        P(("z", "y"), "dp"),
        P(("z", "y"), "dp"),
        P("groups"),
        P("groups"),
        P("groups"),
    )
    return jax.shard_map(
        functools.partial(on_device, groups, zs, ys),
        mesh=fine,
        in_specs=placed,
        out_specs=P(("groups", "z", "y", "dp"), None),
        check_vma=False,
    )
```

```python
import functools

import jax
import jax.numpy as jnp
from jax import lax
from jax.experimental import pallas as pl
from jax.experimental.pallas import tpu as pltpu
from jax.sharding import Mesh
from jax.sharding import PartitionSpec as P

HEAD = 128
BLOCK = 128
CHUNK_HEADS = (2, 2)
MIB = 1024 * 1024
COST = pl.CostEstimate(flops=1, bytes_accessed=1, transcendentals=0)


def rollout_info(positions, lengths, overlong):
    ends = jnp.cumsum(lengths)
    starts = ends - lengths
    which = jnp.sum((ends[None, :] <= positions[:, None]).astype(jnp.int32), axis=1)
    match = jnp.arange(lengths.shape[0], dtype=jnp.int32)[None, :] == which[:, None]
    offset = positions - jnp.sum(jnp.where(match, starts[None, :], 0), axis=1)
    masked = jnp.sum(jnp.where(match, overlong[None, :], 0), axis=1)
    return (which, offset, masked)


def rotation(offset):
    half = HEAD // 2
    freqs = jnp.power(
        jnp.float32(500000.0), -jnp.arange(half, dtype=jnp.float32) * 2.0 / HEAD
    )
    angle = offset.astype(jnp.float32)[:, None] * freqs[None, :]
    cosine, sine = jnp.cos(angle), jnp.sin(angle)
    return jnp.concatenate([cosine, cosine], axis=1), jnp.concatenate([-sine, sine], axis=1)


def shift_square(block, dx, dy, groups, ys):
    route = [
        (x * ys + y, (x + dx) % groups * ys + (y + dy) % ys)
        for x in range(groups)
        for y in range(ys)
    ]
    return lax.ppermute(block, ("groups", "y"), route)


def swap_core(block):
    return lax.ppermute(block, "dp", [(0, 1), (1, 0)])


def after(block, *done):
    return lax.optimization_barrier((block, *done))[0]


def hop_down(block, step, zs):
    with jax.named_scope("hop%d_down" % step):
        return lax.ppermute(block, "z", [(i, i - 1) for i in range(1, zs - step + 1)])


def hop_up(block, step, zs):
    with jax.named_scope("hop%d_up" % step):
        return lax.ppermute(block, "z", [(i, i + 1) for i in range(step - 1, zs - 1)])


def hop_ends(block, zs):
    with jax.named_scope("hop_ends"):
        return lax.ppermute(block, "z", [(1, 0), (zs - 2, zs - 1)])


def nearest(z, place, zs):
    low = jnp.minimum(z, zs - 1 - z)
    step = (place + 1) // 2
    inner = z - step if place % 2 else z + step
    return jnp.where(place <= 2 * low, inner, jnp.where(2 * z < zs, place, zs - 1 - place))


def ways(place, zs):
    if place == 0:
        return [(None, "own", 0)]
    step = (place + 1) // 2
    inner = [(None, "up" if place % 2 else "down", step)] if place <= zs - 2 else []
    ends = [z for z in range(zs // 2) if 2 * z < place]
    return (
        inner
        + [(z, "down", place - z) for z in ends]
        + [(zs - 1 - z, "up", place - z) for z in ends]
    )


def norm_kernel(zs, ys, groups, width, tokens, gain, out):
    z = lax.axis_index("z")
    rows, columns = tokens.shape
    step = min(columns, 1024)
    squares = jnp.zeros((rows, step), jnp.float32)
    for at in range(0, columns, step):
        part = tokens[:, at : at + step].astype(jnp.float32)
        squares += part * part
    factor = lax.rsqrt(jnp.sum(squares, axis=1, keepdims=True) / columns + 1e-05)
    for s in range(zs):
        into = slice(s * width, (s + 1) * width)
        for peer in range(groups * ys):
            x, y = peer // ys, peer % ys
            blk = nearest(z, s, zs) * ys + y
            start = pl.multiple_of((blk * groups + x) * width, width)
            part = tokens[:, pl.ds(start, width)].astype(jnp.float32)
            scale = gain[:, pl.ds(start, width)]
            out[peer, :, into] = (part * factor * scale).astype(jnp.bfloat16)


def norm_pieces(tokens, gain, zs, ys, groups, width):
    count, columns = tokens.shape
    rows = min(count, 32)
    shape = (groups * ys, count, zs * width)
    return pl.pallas_call(
        functools.partial(norm_kernel, zs, ys, groups, width),
        grid=(count // rows,),
        in_specs=[
            pl.BlockSpec((rows, columns), lambda i: (i, 0)),
            pl.BlockSpec((1, columns), lambda i: (0, 0)),
        ],
        out_specs=pl.BlockSpec((shape[0], rows, shape[2]), lambda i: (0, i, 0)),
        out_shape=jax.ShapeDtypeStruct(shape, jnp.bfloat16),
        compiler_params=pltpu.CompilerParams(vmem_limit_bytes=24 * MIB),
        cost_estimate=COST,
        name="norm",
    )(tokens, gain.astype(jnp.float32)[None, :])


def peer_order(ys, groups, peers):
    x, y = lax.axis_index("groups"), lax.axis_index("y")
    return [
        lax.rem(x + (groups - peer // ys), groups) * ys + lax.rem(y + (ys - peer % ys), ys)
        for peer in range(peers)
    ]


def collect_kernel(zs, ys, groups, names, cuts, *refs):
    mine, others = refs[:2]
    weights, outs = dict(zip(names, refs[2:])), refs[2 + len(names) :]
    z = lax.axis_index("z")
    base, size = cuts[0][0], sum(size for _, size in cuts)
    peers, _, columns = mine.shape
    width = columns // zs
    index = peer_order(ys, groups, peers)
    total = None
    for place in range(zs):
        into = slice(place * width, (place + 1) * width)
        rows = jnp.concatenate([ref[i, :, into] for ref in (mine, others) for i in index], axis=0)
        weight = None
        for who, way, hops in ways(place, zs):
            if (way, hops) in weights:
                read = weights[way, hops][:, base : base + size]
                if weight is None:
                    weight = read if who is None else jnp.where(z == who, read, jnp.zeros_like(read))
                else:
                    weight = jnp.where(z == who, read, weight)
        product = jnp.dot(rows, weight, preferred_element_type=jnp.float32)
        total = product if total is None else total + product
    for (first, size), out in zip(cuts, outs):
        out[...] = total[:, first - base : first - base + size]


def collect(mine, others, pieces, cuts, zs, ys, groups):
    rows = 2 * mine.shape[0] * mine.shape[1]
    operands = [mine, others, *pieces.values()]
    return pl.pallas_call(
        functools.partial(collect_kernel, zs, ys, groups, list(pieces), cuts),
        in_specs=[pl.BlockSpec(memory_space=pltpu.VMEM)] * len(operands),
        out_specs=[pl.BlockSpec(memory_space=pltpu.VMEM)] * len(cuts),
        out_shape=[jax.ShapeDtypeStruct((rows, size), jnp.float32) for _, size in cuts],
        compiler_params=pltpu.CompilerParams(vmem_limit_bytes=40 * MIB),
        cost_estimate=COST,
        name="collect",
    )(*operands)


def finish_kernel(ys, groups, layout, mine, others, last, sums, *outs):
    side = lax.axis_index("dp")
    peers, count = mine.shape[:2]
    index = peer_order(ys, groups, peers)
    rows = jnp.concatenate([ref[i] for ref in (mine, others) for i in index], axis=0)
    total = sums[...] + jnp.dot(rows, last[...], preferred_element_type=jnp.float32)
    here = pl.multiple_of(side * count, count)
    there = pl.multiple_of((1 - side) * count, count)
    for (first, size, which), out in zip(layout, outs):
        part = total[:, first : first + size]
        for at, peer in enumerate(which):
            out[at, pl.ds(here, count), :] = part[peer * count : (peer + 1) * count]
            out[at, pl.ds(there, count), :] = part[(peers + peer) * count : (peers + peer + 1) * count]


def finish(mine, others, last, sums, layout, ys, groups):
    peers, count, columns = mine.shape
    width = last.shape[0]
    tokens = pl.BlockSpec((peers, count, width), lambda i: (0, 0, columns // width - 1))
    shapes = [(len(which), 2 * count, size) for _, size, which in layout]
    return pl.pallas_call(
        functools.partial(finish_kernel, ys, groups, layout),
        grid=(1,),
        in_specs=[
            tokens,
            tokens,
            pl.BlockSpec(last.shape, lambda i: (0, 0)),
            pl.BlockSpec(sums.shape, lambda i: (0, 0)),
        ],
        out_specs=[pl.BlockSpec(shape, lambda i: (0, 0, 0)) for shape in shapes],
        out_shape=[jax.ShapeDtypeStruct(shape, jnp.float32) for shape in shapes],
        compiler_params=pltpu.CompilerParams(vmem_limit_bytes=32 * MIB),
        cost_estimate=COST,
        name="finish",
    )(mine, others, last, sums)


def attend_kernel(peers, window, place, *refs):
    partials = refs[:peers]
    cosine, sine, query_info, which_key, here, there, kept, sent = refs[peers:]
    side, own_slot, other_slot, first = place[0], place[1], place[2], place[3]
    rows = cosine.shape[0]
    spots = [place[4 + i] for i in range(window // rows)]
    here, there = (
        jnp.concatenate([ref[pl.ds(pl.multiple_of(at, rows), rows), :] for at in spots], axis=0)
        for ref in (here, there)
    )
    key = jnp.where(side == 0, here, there)
    value = jnp.where(side == 0, there, here)
    which, position, masked = query_info[:, 0:1], query_info[:, 1:2], query_info[:, 2:3]
    key_position = first + lax.broadcasted_iota(jnp.int32, (1, window), 1)
    valid = (which == which_key[...]) & (key_position <= position)
    proj = partials[0][...]
    for other in partials[1:]:
        proj = proj + other[...]
    turned = proj * cosine[...] + pltpu.roll(proj, HEAD // 2, 1) * sine[...]
    scores = lax.dot_general(
        turned.astype(jnp.bfloat16), key, (((1,), (1,)), ((), ())), preferred_element_type=jnp.float32
    ) * HEAD ** (-0.5)
    largest = jnp.max(jnp.where(valid, scores, -1e30), axis=1, keepdims=True)
    weights = jnp.where(valid, jnp.exp(scores - largest), 0.0)
    total = jnp.sum(weights, axis=1, keepdims=True)
    summed = jnp.dot(weights.astype(jnp.bfloat16), value, preferred_element_type=jnp.float32)
    out = jnp.where(masked == 1, 0.0, summed / total).astype(jnp.bfloat16)
    low, high = out[:BLOCK], out[BLOCK:]
    kept[...] = jnp.where(own_slot == 0, low, high)
    sent[...] = jnp.where(other_slot == 0, low, high)


def attend(partials, cosine, sine, query_info, which_key, here, there, place):
    rows, window = cosine.shape[0], which_key.shape[1]
    heads = partials[0].shape[1] // HEAD
    fixed = [cosine, sine, query_info, which_key, here, there]
    return pl.pallas_call(
        functools.partial(attend_kernel, len(partials), window),
        grid=(heads,),
        in_specs=[pl.BlockSpec(memory_space=pltpu.SMEM)]
        + [pl.BlockSpec((rows, HEAD), lambda h: (0, h))] * len(partials)
        + [pl.BlockSpec(array.shape, lambda h: (0, 0)) for array in fixed],
        out_specs=[pl.BlockSpec((BLOCK, HEAD), lambda h: (0, h))] * 2,
        out_shape=[jax.ShapeDtypeStruct((BLOCK, heads * HEAD), jnp.bfloat16)] * 2,
        compiler_params=pltpu.CompilerParams(vmem_limit_bytes=16 * MIB + 24 * rows * window),
        cost_estimate=COST,
        name="attend",
    )(place, *partials, *fixed)


def on_device(groups, zs, ys, tokens, gain, w_query, w_kv, lengths, overlong, assign):
    count = tokens.shape[0]
    pair = 2 * count
    x, z, y, side = (lax.axis_index(name) for name in ("groups", "z", "y", "dp"))
    blk = z * ys + y
    width = w_query.shape[0] // groups
    peers = [(dx, dy) for dx in range(groups) for dy in range(ys)]
    pair_base = blk * pair
    block_base = pair_base // BLOCK
    slots = lax.dynamic_slice_in_dim(assign, block_base, 2) - block_base
    own_slot = lax.dynamic_index_in_dim(slots, side, keepdims=False)
    other_slot = lax.dynamic_index_in_dim(slots, 1 - side, keepdims=False)
    tokens_all = zs * ys * pair
    window = min(tokens_all // 2 + pair, tokens_all)
    first_key = jnp.maximum(pair_base - tokens_all // 2, 0)
    key_blk = first_key // pair + jnp.arange(window // pair, dtype=jnp.int32)
    spot = (blk % ys + ys - key_blk % ys) % ys + (z + zs - key_blk // ys) % zs * ys
    place = jnp.concatenate(
        [jnp.stack([side, own_slot, other_slot, first_key]).astype(jnp.int32), spot * pair]
    )

    own = jnp.concatenate(
        [
            lax.dynamic_slice_in_dim(w_kv, x * width, width, 0),
            lax.dynamic_slice_in_dim(w_query, x * width, width, 0),
        ],
        axis=1,
    )
    normed = norm_pieces(tokens, gain, zs, ys, groups, width)
    pair_rows = pair_base + jnp.arange(pair, dtype=jnp.int32)
    which, offset, masked = rollout_info(pair_rows, lengths, overlong)
    cosine, sine = rotation(offset)
    query_info = jnp.stack([which, pair_rows, masked], axis=1)
    key_place = first_key + jnp.arange(window, dtype=jnp.int32)
    ends = jnp.cumsum(lengths)
    which_key = jnp.sum((ends[:, None] <= key_place[None, :]).astype(jnp.int32), axis=0)[None, :]
    tables = (cosine, sine, query_info, which_key, place)

    mine = lax.all_to_all(normed, ("groups", "y"), 0, 0, tiled=True)
    pieces = {("own", 0): own}
    came = [after(own, normed), after(own, normed)]
    for step in range(1, zs - 1):
        came = [hop_down(came[0], step, zs), hop_up(came[1], step, zs)]
        pieces["down", step], pieces["up", step] = came
    done = (mine, *came, *tables)
    others = swap_core(after(mine, *done))
    came = [after(came[0], *done), after(came[1], *done)]
    cosine, sine, query_info, which_key, place = lax.optimization_barrier((*tables, mine))[:5]
    cuts, first = [(0, HEAD)], HEAD
    for heads in CHUNK_HEADS:
        cuts.append((first, heads * HEAD))
        first += heads * HEAD
    parts = [cuts[0], (HEAD, own.shape[1] - HEAD)]
    last = [
        hop_ends(jnp.where(z == 1, came[0][:, a : a + n], came[1][:, a : a + n]), zs)
        for a, n in parts
    ]
    sums = [collect(mine, others, pieces, [part], zs, ys, groups)[0] for part in parts]

    def to_owner(part, dx, dy):
        return shift_square(part, -dx, -dy, groups, ys) if dx or dy else part

    layout = [(0, HEAD, [at]) for at in range(len(peers))]
    kv_parts = finish(mine, others, last[0], sums[0], layout, ys, groups)
    proj = sum(to_owner(part[0], *peer) for part, peer in zip(kv_parts, peers))
    turned = proj * cosine + jnp.roll(proj, HEAD // 2, axis=1) * sine
    kept_kv = jnp.where(side == 0, turned, proj).astype(jnp.bfloat16)
    kept_kv, last[1] = lax.optimization_barrier((kept_kv, last[1]))
    beside = lax.ppermute(kept_kv, "y", [(i, (i + 1) % ys) for i in range(ys)])

    split = CHUNK_HEADS[0] * HEAD
    rest = CHUNK_HEADS[1] * HEAD
    layout = [(0, split, [dx * ys + dy for dy in range(ys)]) for dx in range(groups)]
    layout += [(split, rest, [dx * ys + dy for dx in range(groups)]) for dy in range(ys)]
    parts = finish(mine, others, last[1], sums[1], layout, ys, groups)
    beside, *parts = lax.optimization_barrier((beside, *parts))
    by_group = sum(to_owner(part, dx, 0) for dx, part in enumerate(parts[:groups]))
    by_y = sum(to_owner(part, 0, dy) for dy, part in enumerate(parts[groups:]))
    partials = [
        [to_owner(by_group[dy], 0, dy) for dy in range(ys)],
        [to_owner(by_y[dx], dx, 0) for dx in range(groups)],
    ]

    both = jnp.concatenate([kept_kv, beside], axis=0)
    along = [both] + [
        lax.ppermute(both, "z", [(i, (i + n) % zs) for i in range(zs)]) for n in range(1, zs)
    ]
    here = jnp.concatenate(along, axis=0)
    there = swap_core(here)

    kept, got = [], []
    for part in partials:
        owned, other = attend(part, cosine, sine, query_info, which_key, here, there, place)
        kept.append(owned)
        got.append(swap_core(other))
    kept = jnp.concatenate(kept, axis=1)
    got = jnp.concatenate(got, axis=1)
    return jnp.where(
        side == 0,
        jnp.concatenate([kept, got], axis=1),
        jnp.concatenate([got, kept], axis=1),
    )


def solution(mesh):
    groups, blks, cores = (mesh.shape[name] for name in ("groups", "blk", "dp"))
    ys = 2
    zs = blks // ys
    fine = Mesh(mesh.devices.reshape(groups, zs, ys, cores), ("groups", "z", "y", "dp"))
    placed = (
        P(("groups", "z", "y", "dp"), None),
        P(),
        P(("z", "y"), "dp"),
        P(("z", "y"), "dp"),
        P("groups"),
        P("groups"),
        P("groups"),
    )
    return jax.shard_map(
        functools.partial(on_device, groups, zs, ys),
        mesh=fine,
        in_specs=placed,
        out_specs=P(("groups", "z", "y", "dp"), None),
        check_vma=False,
    )
```

```python
import functools

import jax
import jax.numpy as jnp
from jax import lax
from jax.experimental import pallas as pl
from jax.experimental.pallas import tpu as pltpu
from jax.sharding import Mesh
from jax.sharding import PartitionSpec as P

HEAD = 128
BLOCK = 128
CHUNK_HEADS = (2, 2)
MIB = 1024 * 1024
COST = pl.CostEstimate(flops=1, bytes_accessed=1, transcendentals=0)


def rollout_info(positions, lengths, overlong):
    ends = jnp.cumsum(lengths)
    starts = ends - lengths
    which = jnp.sum((ends[None, :] <= positions[:, None]).astype(jnp.int32), axis=1)
    match = jnp.arange(lengths.shape[0], dtype=jnp.int32)[None, :] == which[:, None]
    offset = positions - jnp.sum(jnp.where(match, starts[None, :], 0), axis=1)
    masked = jnp.sum(jnp.where(match, overlong[None, :], 0), axis=1)
    return (which, offset, masked)


def rotation(offset):
    half = HEAD // 2
    freqs = jnp.power(
        jnp.float32(500000.0), -jnp.arange(half, dtype=jnp.float32) * 2.0 / HEAD
    )
    angle = offset.astype(jnp.float32)[:, None] * freqs[None, :]
    cosine, sine = jnp.cos(angle), jnp.sin(angle)
    return jnp.concatenate([cosine, cosine], axis=1), jnp.concatenate([-sine, sine], axis=1)


def shift_square(block, dx, dy, groups, ys):
    route = [
        (x * ys + y, (x + dx) % groups * ys + (y + dy) % ys)
        for x in range(groups)
        for y in range(ys)
    ]
    return lax.ppermute(block, ("groups", "y"), route)


def swap_core(block):
    return lax.ppermute(block, "dp", [(0, 1), (1, 0)])


def after(block, *done):
    return lax.optimization_barrier((block, *done))[0]


def hop_down(block, step, zs):
    with jax.named_scope("hop%d_down" % step):
        return lax.ppermute(block, "z", [(i, i - 1) for i in range(1, zs - step + 1)])


def hop_up(block, step, zs):
    with jax.named_scope("hop%d_up" % step):
        return lax.ppermute(block, "z", [(i, i + 1) for i in range(step - 1, zs - 1)])


def hop_ends(block, zs):
    with jax.named_scope("hop_ends"):
        return lax.ppermute(block, "z", [(1, 0), (zs - 2, zs - 1)])


def nearest(z, place, zs):
    low = jnp.minimum(z, zs - 1 - z)
    step = (place + 1) // 2
    inner = z - step if place % 2 else z + step
    return jnp.where(place <= 2 * low, inner, jnp.where(2 * z < zs, place, zs - 1 - place))


def ways(place, zs):
    if place == 0:
        return [(None, "own", 0)]
    step = (place + 1) // 2
    inner = [(None, "up" if place % 2 else "down", step)] if place <= zs - 2 else []
    ends = [z for z in range(zs // 2) if 2 * z < place]
    return (
        inner
        + [(z, "down", place - z) for z in ends]
        + [(zs - 1 - z, "up", place - z) for z in ends]
    )


def norm_kernel(zs, ys, groups, width, tokens, gain, near, *far):
    x, z, y = (lax.axis_index(name) for name in ("groups", "z", "y"))
    rows, columns = tokens.shape
    step = min(columns, 1024)
    squares = jnp.zeros((rows, step), jnp.float32)
    for at in range(0, columns, step):
        part = tokens[:, at : at + step].astype(jnp.float32)
        squares += part * part
    factor = lax.rsqrt(jnp.sum(squares, axis=1, keepdims=True) / columns + 1e-05)
    half = zs // 2
    for s in range(zs):
        into = slice(s % half * width, (s % half + 1) * width)
        for peer in range(groups * ys):
            to_x, to_y = peer // ys, peer % ys
            if s >= half:
                to_x, to_y = lax.rem(x + to_x, groups), lax.rem(y + to_y, ys)
            blk = nearest(z, s, zs) * ys + to_y
            start = pl.multiple_of((blk * groups + to_x) * width, width)
            part = tokens[:, pl.ds(start, width)].astype(jnp.float32)
            scale = gain[:, pl.ds(start, width)]
            out = near.at[peer] if s < half else far[peer]
            out[:, into] = (part * factor * scale).astype(jnp.bfloat16)


def norm_pieces(tokens, gain, zs, ys, groups, width):
    count, columns = tokens.shape
    rows = min(count, 32)
    shape = (groups * ys, count, zs // 2 * width)
    return pl.pallas_call(
        functools.partial(norm_kernel, zs, ys, groups, width),
        grid=(count // rows,),
        in_specs=[
            pl.BlockSpec((rows, columns), lambda i: (i, 0)),
            pl.BlockSpec((1, columns), lambda i: (0, 0)),
        ],
        out_specs=[pl.BlockSpec((shape[0], rows, shape[2]), lambda i: (0, i, 0))]
        + [pl.BlockSpec((rows, shape[2]), lambda i: (i, 0))] * shape[0],
        out_shape=[jax.ShapeDtypeStruct(shape, jnp.bfloat16)]
        + [jax.ShapeDtypeStruct(shape[1:], jnp.bfloat16)] * shape[0],
        compiler_params=pltpu.CompilerParams(vmem_limit_bytes=24 * MIB),
        cost_estimate=COST,
        name="norm",
    )(tokens, gain.astype(jnp.float32)[None, :])


def peer_order(ys, groups, peers):
    x, y = lax.axis_index("groups"), lax.axis_index("y")
    return [
        lax.rem(x + (groups - peer // ys), groups) * ys + lax.rem(y + (ys - peer % ys), ys)
        for peer in range(peers)
    ]


def collect_kernel(zs, ys, groups, names, cuts, *refs):
    mine, others = refs[:2], refs[2:4]
    weights, outs = dict(zip(names, refs[4:])), refs[4 + len(names) :]
    z = lax.axis_index("z")
    base, size = cuts[0][0], sum(size for _, size in cuts)
    peers, _, columns = mine[0].shape
    half = zs // 2
    width = columns // half
    orders = peer_order(ys, groups, peers), range(peers)
    total = None
    for place in range(zs):
        part, at = place // half, place % half * width
        rows = jnp.concatenate(
            [ref[part][i, :, at : at + width] for ref in (mine, others) for i in orders[part]], axis=0
        )
        weight = None
        for who, way, hops in ways(place, zs):
            if (way, hops) in weights:
                read = weights[way, hops][:, base : base + size]
                if weight is None:
                    weight = read if who is None else jnp.where(z == who, read, jnp.zeros_like(read))
                else:
                    weight = jnp.where(z == who, read, weight)
        product = jnp.dot(rows, weight, preferred_element_type=jnp.float32)
        total = product if total is None else total + product
    for (first, size), out in zip(cuts, outs):
        out[...] = total[:, first - base : first - base + size]


def collect(mine, others, pieces, cuts, zs, ys, groups):
    rows = 2 * mine[0].shape[0] * mine[0].shape[1]
    operands = [*mine, *others, *pieces.values()]
    return pl.pallas_call(
        functools.partial(collect_kernel, zs, ys, groups, list(pieces), cuts),
        in_specs=[pl.BlockSpec(memory_space=pltpu.VMEM)] * len(operands),
        out_specs=[pl.BlockSpec(memory_space=pltpu.VMEM)] * len(cuts),
        out_shape=[jax.ShapeDtypeStruct((rows, size), jnp.float32) for _, size in cuts],
        compiler_params=pltpu.CompilerParams(vmem_limit_bytes=40 * MIB),
        cost_estimate=COST,
        name="collect",
    )(*operands)


def finish_kernel(layout, mine, others, last, sums, *outs):
    side = lax.axis_index("dp")
    peers, count = mine.shape[:2]
    rows = jnp.concatenate(
        [ref[...].reshape(peers * count, ref.shape[2]) for ref in (mine, others)], axis=0
    )
    total = sums[...] + jnp.dot(rows, last[...], preferred_element_type=jnp.float32)
    here = pl.multiple_of(side * count, count)
    there = pl.multiple_of((1 - side) * count, count)
    for (first, size, which), out in zip(layout, outs):
        part = total[:, first : first + size]
        for at, peer in enumerate(which):
            out[at, pl.ds(here, count), :] = part[peer * count : (peer + 1) * count]
            out[at, pl.ds(there, count), :] = part[(peers + peer) * count : (peers + peer + 1) * count]


def finish(mine, others, last, sums, layout):
    peers, count, columns = mine.shape
    width = last.shape[0]
    tokens = pl.BlockSpec((peers, count, width), lambda i: (0, 0, columns // width - 1))
    shapes = [(len(which), 2 * count, size) for _, size, which in layout]
    return pl.pallas_call(
        functools.partial(finish_kernel, layout),
        grid=(1,),
        in_specs=[
            tokens,
            tokens,
            pl.BlockSpec(last.shape, lambda i: (0, 0)),
            pl.BlockSpec(sums.shape, lambda i: (0, 0)),
        ],
        out_specs=[pl.BlockSpec(shape, lambda i: (0, 0, 0)) for shape in shapes],
        out_shape=[jax.ShapeDtypeStruct(shape, jnp.float32) for shape in shapes],
        compiler_params=pltpu.CompilerParams(vmem_limit_bytes=32 * MIB),
        cost_estimate=COST,
        name="finish",
    )(mine, others, last, sums)


def attend_kernel(peers, window, place, *refs):
    partials = refs[:peers]
    cosine, sine, query_info, which_key, here, there, kept, sent = refs[peers:]
    side, own_slot, other_slot, first = place[0], place[1], place[2], place[3]
    rows = cosine.shape[0]
    spots = [place[4 + i] for i in range(window // rows)]
    here, there = (
        jnp.concatenate([ref[pl.ds(pl.multiple_of(at, rows), rows), :] for at in spots], axis=0)
        for ref in (here, there)
    )
    key = jnp.where(side == 0, here, there)
    value = jnp.where(side == 0, there, here)
    which, position, masked = query_info[:, 0:1], query_info[:, 1:2], query_info[:, 2:3]
    key_position = first + lax.broadcasted_iota(jnp.int32, (1, window), 1)
    valid = (which == which_key[...]) & (key_position <= position)
    proj = partials[0][...]
    for other in partials[1:]:
        proj = proj + other[...]
    turned = proj * cosine[...] + pltpu.roll(proj, HEAD // 2, 1) * sine[...]
    scores = lax.dot_general(
        turned.astype(jnp.bfloat16), key, (((1,), (1,)), ((), ())), preferred_element_type=jnp.float32
    ) * HEAD ** (-0.5)
    largest = jnp.max(jnp.where(valid, scores, -1e30), axis=1, keepdims=True)
    weights = jnp.where(valid, jnp.exp(scores - largest), 0.0)
    total = jnp.sum(weights, axis=1, keepdims=True)
    summed = jnp.dot(weights.astype(jnp.bfloat16), value, preferred_element_type=jnp.float32)
    out = jnp.where(masked == 1, 0.0, summed / total).astype(jnp.bfloat16)
    low, high = out[:BLOCK], out[BLOCK:]
    kept[...] = jnp.where(own_slot == 0, low, high)
    sent[...] = jnp.where(other_slot == 0, low, high)


def attend(partials, cosine, sine, query_info, which_key, here, there, place):
    rows, window = cosine.shape[0], which_key.shape[1]
    heads = partials[0].shape[1] // HEAD
    fixed = [cosine, sine, query_info, which_key, here, there]
    return pl.pallas_call(
        functools.partial(attend_kernel, len(partials), window),
        grid=(heads,),
        in_specs=[pl.BlockSpec(memory_space=pltpu.SMEM)]
        + [pl.BlockSpec((rows, HEAD), lambda h: (0, h))] * len(partials)
        + [pl.BlockSpec(array.shape, lambda h: (0, 0)) for array in fixed],
        out_specs=[pl.BlockSpec((BLOCK, HEAD), lambda h: (0, h))] * 2,
        out_shape=[jax.ShapeDtypeStruct((BLOCK, heads * HEAD), jnp.bfloat16)] * 2,
        compiler_params=pltpu.CompilerParams(vmem_limit_bytes=16 * MIB + 24 * rows * window),
        cost_estimate=COST,
        name="attend",
    )(place, *partials, *fixed)


def on_device(groups, zs, ys, tokens, gain, w_query, w_kv, lengths, overlong, assign):
    count = tokens.shape[0]
    pair = 2 * count
    x, z, y, side = (lax.axis_index(name) for name in ("groups", "z", "y", "dp"))
    blk = z * ys + y
    width = w_query.shape[0] // groups
    peers = [(dx, dy) for dx in range(groups) for dy in range(ys)]
    pair_base = blk * pair
    block_base = pair_base // BLOCK
    slots = lax.dynamic_slice_in_dim(assign, block_base, 2) - block_base
    own_slot = lax.dynamic_index_in_dim(slots, side, keepdims=False)
    other_slot = lax.dynamic_index_in_dim(slots, 1 - side, keepdims=False)
    tokens_all = zs * ys * pair
    window = min(tokens_all // 2 + pair, tokens_all)
    first_key = jnp.maximum(pair_base - tokens_all // 2, 0)
    key_blk = first_key // pair + jnp.arange(window // pair, dtype=jnp.int32)
    spot = (blk % ys + ys - key_blk % ys) % ys + (z + zs - key_blk // ys) % zs * ys
    place = jnp.concatenate(
        [jnp.stack([side, own_slot, other_slot, first_key]).astype(jnp.int32), spot * pair]
    )

    own = jnp.concatenate(
        [
            lax.dynamic_slice_in_dim(w_kv, x * width, width, 0),
            lax.dynamic_slice_in_dim(w_query, x * width, width, 0),
        ],
        axis=1,
    )
    normed = norm_pieces(tokens, gain, zs, ys, groups, width)
    pair_rows = pair_base + jnp.arange(pair, dtype=jnp.int32)
    which, offset, masked = rollout_info(pair_rows, lengths, overlong)
    cosine, sine = rotation(offset)
    query_info = jnp.stack([which, pair_rows, masked], axis=1)
    key_place = first_key + jnp.arange(window, dtype=jnp.int32)
    ends = jnp.cumsum(lengths)
    which_key = jnp.sum((ends[:, None] <= key_place[None, :]).astype(jnp.int32), axis=0)[None, :]
    tables = (cosine, sine, query_info, which_key, place)

    near, *far = normed
    near = lax.all_to_all(near, ("groups", "y"), 0, 0, tiled=True)
    pieces = {("own", 0): own}
    came = [own, own]
    for step in range(1, zs - 1):
        came = [hop_down(came[0], step, zs), hop_up(came[1], step, zs)]
        pieces["down", step], pieces["up", step] = came
    far = lax.optimization_barrier((near, *far))[1:]
    far = [
        shift_square(part, dx, dy, groups, ys) if dx or dy else part
        for (dx, dy), part in zip(peers, far)
    ]
    mine = [near, jnp.stack(far)]
    done = (*mine, *came, *tables)
    others = [swap_core(after(half, *done)) for half in mine]
    came = [after(came[0], *done), after(came[1], *done)]
    cosine, sine, query_info, which_key, place = lax.optimization_barrier((*tables, near))[:5]
    cuts, first = [(0, HEAD)], HEAD
    for heads in CHUNK_HEADS:
        cuts.append((first, heads * HEAD))
        first += heads * HEAD
    parts = [cuts[0], (HEAD, own.shape[1] - HEAD)]
    last = [
        hop_ends(jnp.where(z == 1, came[0][:, a : a + n], came[1][:, a : a + n]), zs)
        for a, n in parts
    ]
    sums = [collect(mine, others, pieces, [part], zs, ys, groups)[0] for part in parts]

    def to_owner(part, dx, dy):
        return shift_square(part, -dx, -dy, groups, ys) if dx or dy else part

    layout = [(0, HEAD, [at]) for at in range(len(peers))]
    kv_parts = finish(mine[1], others[1], last[0], sums[0], layout)
    proj = sum(to_owner(part[0], *peer) for part, peer in zip(kv_parts, peers))
    turned = proj * cosine + jnp.roll(proj, HEAD // 2, axis=1) * sine
    kept_kv = jnp.where(side == 0, turned, proj).astype(jnp.bfloat16)
    kept_kv, last[1] = lax.optimization_barrier((kept_kv, last[1]))
    beside = lax.ppermute(kept_kv, "y", [(i, (i + 1) % ys) for i in range(ys)])

    split = CHUNK_HEADS[0] * HEAD
    rest = CHUNK_HEADS[1] * HEAD
    layout = [(0, split, [dx * ys + dy for dy in range(ys)]) for dx in range(groups)]
    layout += [(split, rest, [dx * ys + dy for dx in range(groups)]) for dy in range(ys)]
    parts = finish(mine[1], others[1], last[1], sums[1], layout)
    beside, *parts = lax.optimization_barrier((beside, *parts))
    by_group = sum(to_owner(part, dx, 0) for dx, part in enumerate(parts[:groups]))
    by_y = sum(to_owner(part, 0, dy) for dy, part in enumerate(parts[groups:]))
    partials = [
        [to_owner(by_group[dy], 0, dy) for dy in range(ys)],
        [to_owner(by_y[dx], dx, 0) for dx in range(groups)],
    ]

    both = jnp.concatenate([kept_kv, beside], axis=0)
    along = [both] + [
        lax.ppermute(both, "z", [(i, (i + n) % zs) for i in range(zs)]) for n in range(1, zs)
    ]
    here = jnp.concatenate(along, axis=0)
    there = swap_core(here)

    kept, got = [], []
    for part in partials:
        owned, other = attend(part, cosine, sine, query_info, which_key, here, there, place)
        kept.append(owned)
        got.append(swap_core(other))
    kept = jnp.concatenate(kept, axis=1)
    got = jnp.concatenate(got, axis=1)
    return jnp.where(
        side == 0,
        jnp.concatenate([kept, got], axis=1),
        jnp.concatenate([got, kept], axis=1),
    )


def solution(mesh):
    groups, blks, cores = (mesh.shape[name] for name in ("groups", "blk", "dp"))
    ys = 2
    zs = blks // ys
    fine = Mesh(mesh.devices.reshape(groups, zs, ys, cores), ("groups", "z", "y", "dp"))
    placed = (
        P(("groups", "z", "y", "dp"), None),
        P(),
        P(("z", "y"), "dp"),
        P(("z", "y"), "dp"),
        P("groups"),
        P("groups"),
        P("groups"),
    )
    return jax.shard_map(
        functools.partial(on_device, groups, zs, ys),
        mesh=fine,
        in_specs=placed,
        out_specs=P(("groups", "z", "y", "dp"), None),
        check_vma=False,
    )
```

```python
import functools

import jax
import jax.numpy as jnp
from jax import lax
from jax.experimental import pallas as pl
from jax.experimental.pallas import tpu as pltpu
from jax.sharding import Mesh
from jax.sharding import PartitionSpec as P

HEAD = 128
BLOCK = 128
CHUNK_HEADS = (2, 2)
MIB = 1024 * 1024
COST = pl.CostEstimate(flops=1, bytes_accessed=1, transcendentals=0)


def rollout_info(positions, lengths, overlong):
    ends = jnp.cumsum(lengths)
    starts = ends - lengths
    which = jnp.sum((ends[None, :] <= positions[:, None]).astype(jnp.int32), axis=1)
    match = jnp.arange(lengths.shape[0], dtype=jnp.int32)[None, :] == which[:, None]
    offset = positions - jnp.sum(jnp.where(match, starts[None, :], 0), axis=1)
    masked = jnp.sum(jnp.where(match, overlong[None, :], 0), axis=1)
    return (which, offset, masked)


def rotation(offset):
    half = HEAD // 2
    freqs = jnp.power(
        jnp.float32(500000.0), -jnp.arange(half, dtype=jnp.float32) * 2.0 / HEAD
    )
    angle = offset.astype(jnp.float32)[:, None] * freqs[None, :]
    cosine, sine = jnp.cos(angle), jnp.sin(angle)
    return jnp.concatenate([cosine, cosine], axis=1), jnp.concatenate([-sine, sine], axis=1)


def shift_square(block, dx, dy, groups, ys):
    route = [
        (x * ys + y, (x + dx) % groups * ys + (y + dy) % ys)
        for x in range(groups)
        for y in range(ys)
    ]
    return lax.ppermute(block, ("groups", "y"), route)


def swap_core(block):
    return lax.ppermute(block, "dp", [(0, 1), (1, 0)])


def after(block, *done):
    return lax.optimization_barrier((block, *done))[0]


def hop_down(block, step, zs):
    with jax.named_scope("hop%d_down" % step):
        return lax.ppermute(block, "z", [(i, i - 1) for i in range(1, zs - step + 1)])


def hop_up(block, step, zs):
    with jax.named_scope("hop%d_up" % step):
        return lax.ppermute(block, "z", [(i, i + 1) for i in range(step - 1, zs - 1)])


def hop_ends(block, zs):
    with jax.named_scope("hop_ends"):
        return lax.ppermute(block, "z", [(1, 0), (zs - 2, zs - 1)])


def nearest(z, place, zs):
    low = jnp.minimum(z, zs - 1 - z)
    step = (place + 1) // 2
    inner = z - step if place % 2 else z + step
    return jnp.where(place <= 2 * low, inner, jnp.where(2 * z < zs, place, zs - 1 - place))


def ways(place, zs):
    if place == 0:
        return [(None, "own", 0)]
    if zs == 4:
        return [
            [(None, "pair", 1), (2, "pair", 2)],
            [(None, "pair", 4), (1, "pair", 2), (2, "pair", 1)],
            [(0, "last", 0), (1, "pair", 3), (2, "pair", 3), (3, "last", 0)],
        ][place - 1]
    step = (place + 1) // 2
    inner = [(None, "up" if place % 2 else "down", step)] if place <= zs - 2 else []
    ends = [z for z in range(zs // 2) if 2 * z < place]
    return (
        inner
        + [(z, "down", place - z) for z in ends]
        + [(zs - 1 - z, "up", place - z) for z in ends]
    )


def norm_kernel(zs, ys, groups, width, tokens, gain, near, *far):
    x, z, y = (lax.axis_index(name) for name in ("groups", "z", "y"))
    rows, columns = tokens.shape
    step = min(columns, 1024)
    squares = jnp.zeros((rows, step), jnp.float32)
    for at in range(0, columns, step):
        part = tokens[:, at : at + step].astype(jnp.float32)
        squares += part * part
    factor = lax.rsqrt(jnp.sum(squares, axis=1, keepdims=True) / columns + 1e-05)
    half = zs // 2
    for s in range(zs):
        into = slice(s % half * width, (s % half + 1) * width)
        for peer in range(groups * ys):
            to_x, to_y = peer // ys, peer % ys
            if s >= half:
                to_x, to_y = lax.rem(x + to_x, groups), lax.rem(y + to_y, ys)
            blk = nearest(z, s, zs) * ys + to_y
            start = pl.multiple_of((blk * groups + to_x) * width, width)
            part = tokens[:, pl.ds(start, width)].astype(jnp.float32)
            scale = gain[:, pl.ds(start, width)]
            out = near.at[peer] if s < half else far[peer]
            out[:, into] = (part * factor * scale).astype(jnp.bfloat16)


def norm_pieces(tokens, gain, zs, ys, groups, width):
    count, columns = tokens.shape
    rows = min(count, 32)
    shape = (groups * ys, count, zs // 2 * width)
    return pl.pallas_call(
        functools.partial(norm_kernel, zs, ys, groups, width),
        grid=(count // rows,),
        in_specs=[
            pl.BlockSpec((rows, columns), lambda i: (i, 0)),
            pl.BlockSpec((1, columns), lambda i: (0, 0)),
        ],
        out_specs=[pl.BlockSpec((shape[0], rows, shape[2]), lambda i: (0, i, 0))]
        + [pl.BlockSpec((rows, shape[2]), lambda i: (i, 0))] * shape[0],
        out_shape=[jax.ShapeDtypeStruct(shape, jnp.bfloat16)]
        + [jax.ShapeDtypeStruct(shape[1:], jnp.bfloat16)] * shape[0],
        compiler_params=pltpu.CompilerParams(vmem_limit_bytes=56 * MIB),
        cost_estimate=COST,
        name="norm",
    )(tokens, gain.astype(jnp.float32)[None, :])


def peer_order(ys, groups, peers):
    x, y = lax.axis_index("groups"), lax.axis_index("y")
    return [
        lax.rem(x + (groups - peer // ys), groups) * ys + lax.rem(y + (ys - peer % ys), ys)
        for peer in range(peers)
    ]


def collect_kernel(zs, ys, groups, names, cuts, *refs):
    mine, others = refs[:2], refs[2:4]
    weights, outs = dict(zip(names, refs[4:])), refs[4 + len(names) :]
    z = lax.axis_index("z")
    base, size = cuts[0][0], sum(size for _, size in cuts)
    peers, _, columns = mine[0].shape
    half = zs // 2
    width = columns // half
    orders = peer_order(ys, groups, peers), range(peers)
    total = None
    for place in range(zs):
        part, at = place // half, place % half * width
        rows = jnp.concatenate(
            [ref[part][i, :, at : at + width] for ref in (mine, others) for i in orders[part]], axis=0
        )
        weight = None
        for who, way, hops in ways(place, zs):
            if (way, hops) in weights:
                read = weights[way, hops][:, base : base + size]
                if weight is None:
                    weight = read if who is None else jnp.where(z == who, read, jnp.zeros_like(read))
                else:
                    weight = jnp.where(z == who, read, weight)
        product = jnp.dot(rows, weight, preferred_element_type=jnp.float32)
        total = product if total is None else total + product
    for (first, size), out in zip(cuts, outs):
        out[...] = total[:, first - base : first - base + size]


def collect(mine, others, pieces, cuts, zs, ys, groups):
    rows = 2 * mine[0].shape[0] * mine[0].shape[1]
    operands = [*mine, *others, *pieces.values()]
    return pl.pallas_call(
        functools.partial(collect_kernel, zs, ys, groups, list(pieces), cuts),
        in_specs=[pl.BlockSpec(memory_space=pltpu.VMEM)] * len(operands),
        out_specs=[pl.BlockSpec(memory_space=pltpu.VMEM)] * len(cuts),
        out_shape=[jax.ShapeDtypeStruct((rows, size), jnp.float32) for _, size in cuts],
        compiler_params=pltpu.CompilerParams(vmem_limit_bytes=40 * MIB),
        cost_estimate=COST,
        name="collect",
    )(*operands)


def finish_kernel(layout, mine, others, last, sums, *outs):
    side = lax.axis_index("dp")
    peers, count = mine.shape[:2]
    rows = jnp.concatenate(
        [ref[...].reshape(peers * count, ref.shape[2]) for ref in (mine, others)], axis=0
    )
    total = sums[...] + jnp.dot(rows, last[...], preferred_element_type=jnp.float32)
    here = pl.multiple_of(side * count, count)
    there = pl.multiple_of((1 - side) * count, count)
    for (first, size, which), out in zip(layout, outs):
        part = total[:, first : first + size]
        for at, peer in enumerate(which):
            out[at, pl.ds(here, count), :] = part[peer * count : (peer + 1) * count]
            out[at, pl.ds(there, count), :] = part[(peers + peer) * count : (peers + peer + 1) * count]


def finish(mine, others, last, sums, layout):
    peers, count, columns = mine.shape
    width = last.shape[0]
    tokens = pl.BlockSpec((peers, count, width), lambda i: (0, 0, columns // width - 1))
    shapes = [(len(which), 2 * count, size) for _, size, which in layout]
    return pl.pallas_call(
        functools.partial(finish_kernel, layout),
        grid=(1,),
        in_specs=[
            tokens,
            tokens,
            pl.BlockSpec(last.shape, lambda i: (0, 0)),
            pl.BlockSpec(sums.shape, lambda i: (0, 0)),
        ],
        out_specs=[pl.BlockSpec(shape, lambda i: (0, 0, 0)) for shape in shapes],
        out_shape=[jax.ShapeDtypeStruct(shape, jnp.float32) for shape in shapes],
        compiler_params=pltpu.CompilerParams(vmem_limit_bytes=32 * MIB),
        cost_estimate=COST,
        name="finish",
    )(mine, others, last, sums)


def attend_kernel(peers, window, place, *refs):
    partials = refs[:peers]
    cosine, sine, query_info, which_key, here, there, kept, sent = refs[peers:]
    side, own_slot, other_slot, first = place[0], place[1], place[2], place[3]
    rows = cosine.shape[0]
    spots = [place[4 + i] for i in range(window // rows)]
    here, there = (
        jnp.concatenate([ref[pl.ds(pl.multiple_of(at, rows), rows), :] for at in spots], axis=0)
        for ref in (here, there)
    )
    key = jnp.where(side == 0, here, there)
    value = jnp.where(side == 0, there, here)
    which, position, masked = query_info[:, 0:1], query_info[:, 1:2], query_info[:, 2:3]
    key_position = first + lax.broadcasted_iota(jnp.int32, (1, window), 1)
    valid = (which == which_key[...]) & (key_position <= position)
    proj = partials[0][...]
    for other in partials[1:]:
        proj = proj + other[...]
    turned = proj * cosine[...] + pltpu.roll(proj, HEAD // 2, 1) * sine[...]
    scores = lax.dot_general(
        turned.astype(jnp.bfloat16), key, (((1,), (1,)), ((), ())), preferred_element_type=jnp.float32
    ) * HEAD ** (-0.5)
    largest = jnp.max(jnp.where(valid, scores, -1e30), axis=1, keepdims=True)
    weights = jnp.where(valid, jnp.exp(scores - largest), 0.0)
    total = jnp.sum(weights, axis=1, keepdims=True)
    summed = jnp.dot(weights.astype(jnp.bfloat16), value, preferred_element_type=jnp.float32)
    out = jnp.where(masked == 1, 0.0, summed / total).astype(jnp.bfloat16)
    low, high = out[:BLOCK], out[BLOCK:]
    kept[...] = jnp.where(own_slot == 0, low, high)
    sent[...] = jnp.where(other_slot == 0, low, high)


def attend(partials, cosine, sine, query_info, which_key, here, there, place):
    rows, window = cosine.shape[0], which_key.shape[1]
    heads = partials[0].shape[1] // HEAD
    fixed = [cosine, sine, query_info, which_key, here, there]
    return pl.pallas_call(
        functools.partial(attend_kernel, len(partials), window),
        grid=(heads,),
        in_specs=[pl.BlockSpec(memory_space=pltpu.SMEM)]
        + [pl.BlockSpec((rows, HEAD), lambda h: (0, h))] * len(partials)
        + [pl.BlockSpec(array.shape, lambda h: (0, 0)) for array in fixed],
        out_specs=[pl.BlockSpec((BLOCK, HEAD), lambda h: (0, h))] * 2,
        out_shape=[jax.ShapeDtypeStruct((BLOCK, heads * HEAD), jnp.bfloat16)] * 2,
        compiler_params=pltpu.CompilerParams(vmem_limit_bytes=16 * MIB + 24 * rows * window),
        cost_estimate=COST,
        name="attend",
    )(place, *partials, *fixed)


def on_device(groups, zs, ys, tokens, gain, w_query, w_kv, lengths, overlong, assign):
    count = tokens.shape[0]
    pair = 2 * count
    x, z, y, side = (lax.axis_index(name) for name in ("groups", "z", "y", "dp"))
    blk = z * ys + y
    width = w_query.shape[0] // groups
    peers = [(dx, dy) for dx in range(groups) for dy in range(ys)]
    pair_base = blk * pair
    block_base = pair_base // BLOCK
    slots = lax.dynamic_slice_in_dim(assign, block_base, 2) - block_base
    own_slot = lax.dynamic_index_in_dim(slots, side, keepdims=False)
    other_slot = lax.dynamic_index_in_dim(slots, 1 - side, keepdims=False)
    tokens_all = zs * ys * pair
    window = min(tokens_all // 2 + pair, tokens_all)
    first_key = jnp.maximum(pair_base - tokens_all // 2, 0)
    key_blk = first_key // pair + jnp.arange(window // pair, dtype=jnp.int32)
    spot = (blk % ys + ys - key_blk % ys) % ys + (z + zs - key_blk // ys) % zs * ys
    place = jnp.concatenate(
        [jnp.stack([side, own_slot, other_slot, first_key]).astype(jnp.int32), spot * pair]
    )

    own = jnp.concatenate(
        [
            lax.dynamic_slice_in_dim(w_kv, x * width, width, 0),
            lax.dynamic_slice_in_dim(w_query, x * width, width, 0),
        ],
        axis=1,
    )
    normed = norm_pieces(tokens, gain, zs, ys, groups, width)
    pair_rows = pair_base + jnp.arange(pair, dtype=jnp.int32)
    which, offset, masked = rollout_info(pair_rows, lengths, overlong)
    cosine, sine = rotation(offset)
    query_info = jnp.stack([which, pair_rows, masked], axis=1)
    key_place = first_key + jnp.arange(window, dtype=jnp.int32)
    ends = jnp.cumsum(lengths)
    which_key = jnp.sum((ends[:, None] <= key_place[None, :]).astype(jnp.int32), axis=0)[None, :]
    tables = (cosine, sine, query_info, which_key, place)

    near, *far = normed
    near = lax.all_to_all(near, ("groups", "y"), 0, 0, tiled=True)
    pieces = {("own", 0): own}
    if zs == 4:
        ends, middle = [(0, 1), (1, 0), (2, 3), (3, 2)], [(1, 2), (2, 1)]
        first = [lax.ppermute(own, "z", ends), lax.ppermute(own, "z", middle)]
        came = [lax.ppermute(first[0], "z", middle), lax.ppermute(first[1], "z", [(1, 0), (2, 3)])]
        pieces.update({("pair", 1 + at): block for at, block in enumerate(first + came)})
    else:
        came = [own, own]
        for step in range(1, zs - 1):
            came = [hop_down(came[0], step, zs), hop_up(came[1], step, zs)]
            pieces["down", step], pieces["up", step] = came
    far = lax.optimization_barrier((near, *far))[1:]
    far = [
        shift_square(part, dx, dy, groups, ys) if dx or dy else part
        for (dx, dy), part in zip(peers, far)
    ]
    mine = [near, jnp.stack(far)]
    done = (*mine, *came, *tables)
    others = [swap_core(after(half, *done)) for half in mine]
    came = [after(came[0], *done), after(came[1], *done)]
    cosine, sine, query_info, which_key, place = lax.optimization_barrier((*tables, near))[:5]
    cuts, first = [(0, HEAD)], HEAD
    for heads in CHUNK_HEADS:
        cuts.append((first, heads * HEAD))
        first += heads * HEAD
    parts = [cuts[0], (HEAD, own.shape[1] - HEAD)]
    last = []
    for a, n in parts:
        block = came[0][:, a : a + n]
        if zs != 4:
            block = jnp.where(z == 1, block, came[1][:, a : a + n])
        last.append(hop_ends(block, zs))
    sums = [collect(mine, others, pieces, [part], zs, ys, groups)[0] for part in parts]

    def to_owner(part, dx, dy):
        return shift_square(part, -dx, -dy, groups, ys) if dx or dy else part

    layout = [(0, HEAD, [at]) for at in range(len(peers))]
    kv_parts = finish(mine[1], others[1], last[0], sums[0], layout)
    proj = sum(to_owner(part[0], *peer) for part, peer in zip(kv_parts, peers))
    turned = proj * cosine + jnp.roll(proj, HEAD // 2, axis=1) * sine
    kept_kv = jnp.where(side == 0, turned, proj).astype(jnp.bfloat16)
    kept_kv, last[1] = lax.optimization_barrier((kept_kv, last[1]))
    beside = lax.ppermute(kept_kv, "y", [(i, (i + 1) % ys) for i in range(ys)])

    split = CHUNK_HEADS[0] * HEAD
    rest = CHUNK_HEADS[1] * HEAD
    layout = [(0, split, [dx * ys + dy for dy in range(ys)]) for dx in range(groups)]
    layout += [(split, rest, [dx * ys + dy for dx in range(groups)]) for dy in range(ys)]
    parts = finish(mine[1], others[1], last[1], sums[1], layout)
    beside, *parts = lax.optimization_barrier((beside, *parts))
    by_group = sum(to_owner(part, dx, 0) for dx, part in enumerate(parts[:groups]))
    by_y = sum(to_owner(part, 0, dy) for dy, part in enumerate(parts[groups:]))
    partials = [
        [to_owner(by_group[dy], 0, dy) for dy in range(ys)],
        [to_owner(by_y[dx], dx, 0) for dx in range(groups)],
    ]

    both = jnp.concatenate([kept_kv, beside], axis=0)
    along = [both] + [
        lax.ppermute(both, "z", [(i, (i + n) % zs) for i in range(zs)]) for n in range(1, zs)
    ]
    here = jnp.concatenate(along, axis=0)
    there = swap_core(here)

    kept, got = [], []
    for part in partials:
        owned, other = attend(part, cosine, sine, query_info, which_key, here, there, place)
        kept.append(owned)
        got.append(swap_core(other))
    kept = jnp.concatenate(kept, axis=1)
    got = jnp.concatenate(got, axis=1)
    return jnp.where(
        side == 0,
        jnp.concatenate([kept, got], axis=1),
        jnp.concatenate([got, kept], axis=1),
    )


def solution(mesh):
    groups, blks, cores = (mesh.shape[name] for name in ("groups", "blk", "dp"))
    ys = 2
    zs = blks // ys
    fine = Mesh(mesh.devices.reshape(groups, zs, ys, cores), ("groups", "z", "y", "dp"))
    placed = (
        P(("groups", "z", "y", "dp"), None),
        P(),
        P(("z", "y"), "dp"),
        P(("z", "y"), "dp"),
        P("groups"),
        P("groups"),
        P("groups"),
    )
    return jax.shard_map(
        functools.partial(on_device, groups, zs, ys),
        mesh=fine,
        in_specs=placed,
        out_specs=P(("groups", "z", "y", "dp"), None),
        check_vma=False,
    )
```

```python
import functools

import jax
import jax.numpy as jnp
from jax import lax
from jax.experimental import pallas as pl
from jax.experimental.pallas import tpu as pltpu
from jax.sharding import Mesh
from jax.sharding import PartitionSpec as P

HEAD = 128
BLOCK = 128
CHUNK_HEADS = (2, 2)
MIB = 1024 * 1024
COST = pl.CostEstimate(flops=1, bytes_accessed=1, transcendentals=0)


def rollout_info(positions, lengths, overlong):
    ends = jnp.cumsum(lengths)
    starts = ends - lengths
    which = jnp.sum((ends[None, :] <= positions[:, None]).astype(jnp.int32), axis=1)
    match = jnp.arange(lengths.shape[0], dtype=jnp.int32)[None, :] == which[:, None]
    offset = positions - jnp.sum(jnp.where(match, starts[None, :], 0), axis=1)
    masked = jnp.sum(jnp.where(match, overlong[None, :], 0), axis=1)
    return (which, offset, masked)


def rotation(offset):
    half = HEAD // 2
    freqs = jnp.power(
        jnp.float32(500000.0), -jnp.arange(half, dtype=jnp.float32) * 2.0 / HEAD
    )
    angle = offset.astype(jnp.float32)[:, None] * freqs[None, :]
    cosine, sine = jnp.cos(angle), jnp.sin(angle)
    return jnp.concatenate([cosine, cosine], axis=1), jnp.concatenate([-sine, sine], axis=1)


def shift_square(block, dx, dy, groups, ys):
    route = [
        (x * ys + y, (x + dx) % groups * ys + (y + dy) % ys)
        for x in range(groups)
        for y in range(ys)
    ]
    return lax.ppermute(block, ("groups", "y"), route)


def swap_core(block):
    return lax.ppermute(block, "dp", [(0, 1), (1, 0)])


def after(block, *done):
    return lax.optimization_barrier((block, *done))[0]


def hop_down(block, step, zs):
    with jax.named_scope("hop%d_down" % step):
        return lax.ppermute(block, "z", [(i, i - 1) for i in range(1, zs - step + 1)])


def hop_up(block, step, zs):
    with jax.named_scope("hop%d_up" % step):
        return lax.ppermute(block, "z", [(i, i + 1) for i in range(step - 1, zs - 1)])


def hop_ends(block, zs):
    with jax.named_scope("hop_ends"):
        return lax.ppermute(block, "z", [(1, 0), (zs - 2, zs - 1)])


def nearest(z, place, zs):
    low = jnp.minimum(z, zs - 1 - z)
    step = (place + 1) // 2
    inner = z - step if place % 2 else z + step
    return jnp.where(place <= 2 * low, inner, jnp.where(2 * z < zs, place, zs - 1 - place))


def ways(place, zs):
    if place == 0:
        return [(None, "own", 0)]
    if zs == 4:
        return [
            [(None, "pair", 1), (2, "pair", 2)],
            [(None, "pair", 4), (1, "pair", 2), (2, "pair", 1)],
            [(0, "last", 0), (1, "pair", 3), (2, "pair", 3), (3, "last", 0)],
        ][place - 1]
    step = (place + 1) // 2
    inner = [(None, "up" if place % 2 else "down", step)] if place <= zs - 2 else []
    ends = [z for z in range(zs // 2) if 2 * z < place]
    return (
        inner
        + [(z, "down", place - z) for z in ends]
        + [(zs - 1 - z, "up", place - z) for z in ends]
    )


def norm_kernel(zs, ys, groups, width, tokens, gain, near, *far):
    x, z, y = (lax.axis_index(name) for name in ("groups", "z", "y"))
    rows, columns = tokens.shape
    step = min(columns, 1024)
    squares = jnp.zeros((rows, step), jnp.float32)
    for at in range(0, columns, step):
        part = tokens[:, at : at + step].astype(jnp.float32)
        squares += part * part
    factor = lax.rsqrt(jnp.sum(squares, axis=1, keepdims=True) / columns + 1e-05)
    half = zs // 2
    for s in range(zs):
        into = slice(s % half * width, (s % half + 1) * width)
        for peer in range(groups * ys):
            to_x, to_y = peer // ys, peer % ys
            if s >= half:
                to_x, to_y = lax.rem(x + to_x, groups), lax.rem(y + to_y, ys)
            blk = nearest(z, s, zs) * ys + to_y
            start = pl.multiple_of((blk * groups + to_x) * width, width)
            part = tokens[:, pl.ds(start, width)].astype(jnp.float32)
            scale = gain[:, pl.ds(start, width)]
            out = near.at[peer] if s < half else far[peer]
            out[:, into] = (part * factor * scale).astype(jnp.bfloat16)


def norm_pieces(tokens, gain, zs, ys, groups, width):
    count, columns = tokens.shape
    rows = min(count, 32)
    shape = (groups * ys, count, zs // 2 * width)
    return pl.pallas_call(
        functools.partial(norm_kernel, zs, ys, groups, width),
        grid=(count // rows,),
        in_specs=[
            pl.BlockSpec((rows, columns), lambda i: (i, 0)),
            pl.BlockSpec((1, columns), lambda i: (0, 0)),
        ],
        out_specs=[pl.BlockSpec((shape[0], rows, shape[2]), lambda i: (0, i, 0))]
        + [pl.BlockSpec((rows, shape[2]), lambda i: (i, 0))] * shape[0],
        out_shape=[jax.ShapeDtypeStruct(shape, jnp.bfloat16)]
        + [jax.ShapeDtypeStruct(shape[1:], jnp.bfloat16)] * shape[0],
        compiler_params=pltpu.CompilerParams(vmem_limit_bytes=56 * MIB),
        cost_estimate=COST,
        name="norm",
    )(tokens, gain.astype(jnp.float32)[None, :])


def peer_order(ys, groups, peers):
    x, y = lax.axis_index("groups"), lax.axis_index("y")
    return [
        lax.rem(x + (groups - peer // ys), groups) * ys + lax.rem(y + (ys - peer % ys), ys)
        for peer in range(peers)
    ]


def collect_kernel(zs, ys, groups, names, cuts, *refs):
    mine, others = refs[:2], refs[2:4]
    weights, outs = dict(zip(names, refs[4:])), refs[4 + len(names) :]
    z = lax.axis_index("z")
    base, size = cuts[0][0], sum(size for _, size in cuts)
    peers, _, columns = mine[0].shape
    half = zs // 2
    width = columns // half
    orders = peer_order(ys, groups, peers), range(peers)
    total = None
    for place in range(zs):
        part, at = place // half, place % half * width
        rows = jnp.concatenate(
            [ref[part][i, :, at : at + width] for ref in (mine, others) for i in orders[part]], axis=0
        )
        weight = None
        for who, way, hops in ways(place, zs):
            if (way, hops) in weights:
                read = weights[way, hops][:, base : base + size]
                if weight is None:
                    weight = read if who is None else jnp.where(z == who, read, jnp.zeros_like(read))
                else:
                    weight = jnp.where(z == who, read, weight)
        product = jnp.dot(rows, weight, preferred_element_type=jnp.float32)
        total = product if total is None else total + product
    for (first, size), out in zip(cuts, outs):
        out[...] = total[:, first - base : first - base + size]


def collect(mine, others, pieces, cuts, zs, ys, groups):
    rows = 2 * mine[0].shape[0] * mine[0].shape[1]
    operands = [*mine, *others, *pieces.values()]
    return pl.pallas_call(
        functools.partial(collect_kernel, zs, ys, groups, list(pieces), cuts),
        in_specs=[pl.BlockSpec(memory_space=pltpu.VMEM)] * len(operands),
        out_specs=[pl.BlockSpec(memory_space=pltpu.VMEM)] * len(cuts),
        out_shape=[jax.ShapeDtypeStruct((rows, size), jnp.float32) for _, size in cuts],
        compiler_params=pltpu.CompilerParams(vmem_limit_bytes=40 * MIB),
        cost_estimate=COST,
        name="collect",
    )(*operands)


def finish_kernel(layout, mine, others, last, sums, *outs):
    side = lax.axis_index("dp")
    peers, count = mine.shape[:2]
    rows = jnp.concatenate(
        [ref[...].reshape(peers * count, ref.shape[2]) for ref in (mine, others)], axis=0
    )
    total = sums[...] + jnp.dot(rows, last[...], preferred_element_type=jnp.float32)
    here = pl.multiple_of(side * count, count)
    there = pl.multiple_of((1 - side) * count, count)
    for (first, size, which), out in zip(layout, outs):
        part = total[:, first : first + size]
        for at, peer in enumerate(which):
            out[at, pl.ds(here, count), :] = part[peer * count : (peer + 1) * count]
            out[at, pl.ds(there, count), :] = part[(peers + peer) * count : (peers + peer + 1) * count]


def finish(mine, others, last, sums, layout):
    peers, count, columns = mine.shape
    width = last.shape[0]
    tokens = pl.BlockSpec((peers, count, width), lambda i: (0, 0, columns // width - 1))
    shapes = [(len(which), 2 * count, size) for _, size, which in layout]
    return pl.pallas_call(
        functools.partial(finish_kernel, layout),
        grid=(1,),
        in_specs=[
            tokens,
            tokens,
            pl.BlockSpec(last.shape, lambda i: (0, 0)),
            pl.BlockSpec(sums.shape, lambda i: (0, 0)),
        ],
        out_specs=[pl.BlockSpec(shape, lambda i: (0, 0, 0)) for shape in shapes],
        out_shape=[jax.ShapeDtypeStruct(shape, jnp.float32) for shape in shapes],
        compiler_params=pltpu.CompilerParams(vmem_limit_bytes=32 * MIB),
        cost_estimate=COST,
        name="finish",
    )(mine, others, last, sums)


def attend_kernel(peers, window, place, *refs):
    partials = refs[:peers]
    cosine, sine, query_info, which_key, here, there, kept, sent = refs[peers:]
    side, own_slot, other_slot, first = place[0], place[1], place[2], place[3]
    rows = cosine.shape[0]
    spots = [place[4 + i] for i in range(window // rows)]
    here, there = (
        jnp.concatenate([ref[pl.ds(pl.multiple_of(at, rows), rows), :] for at in spots], axis=0)
        for ref in (here, there)
    )
    key = jnp.where(side == 0, here, there)
    value = jnp.where(side == 0, there, here)
    which, position, masked = query_info[:, 0:1], query_info[:, 1:2], query_info[:, 2:3]
    key_position = first + lax.broadcasted_iota(jnp.int32, (1, window), 1)
    valid = (which == which_key[...]) & (key_position <= position)
    proj = partials[0][...]
    for other in partials[1:]:
        proj = proj + other[...]
    turned = proj * cosine[...] + pltpu.roll(proj, HEAD // 2, 1) * sine[...]
    scores = lax.dot_general(
        turned.astype(jnp.bfloat16), key, (((1,), (1,)), ((), ())), preferred_element_type=jnp.float32
    ) * HEAD ** (-0.5)
    largest = jnp.max(jnp.where(valid, scores, -1e30), axis=1, keepdims=True)
    weights = jnp.where(valid, jnp.exp(scores - largest), 0.0)
    total = jnp.sum(weights, axis=1, keepdims=True)
    summed = jnp.dot(weights.astype(jnp.bfloat16), value, preferred_element_type=jnp.float32)
    out = jnp.where(masked == 1, 0.0, summed / total).astype(jnp.bfloat16)
    low, high = out[:BLOCK], out[BLOCK:]
    kept[...] = jnp.where(own_slot == 0, low, high)
    sent[...] = jnp.where(other_slot == 0, low, high)


def attend(partials, cosine, sine, query_info, which_key, here, there, place):
    rows, window = cosine.shape[0], which_key.shape[1]
    heads = partials[0].shape[1] // HEAD
    fixed = [cosine, sine, query_info, which_key, here, there]
    return pl.pallas_call(
        functools.partial(attend_kernel, len(partials), window),
        grid=(heads,),
        in_specs=[pl.BlockSpec(memory_space=pltpu.SMEM)]
        + [pl.BlockSpec((rows, HEAD), lambda h: (0, h))] * len(partials)
        + [pl.BlockSpec(array.shape, lambda h: (0, 0)) for array in fixed],
        out_specs=[pl.BlockSpec((BLOCK, HEAD), lambda h: (0, h))] * 2,
        out_shape=[jax.ShapeDtypeStruct((BLOCK, heads * HEAD), jnp.bfloat16)] * 2,
        compiler_params=pltpu.CompilerParams(vmem_limit_bytes=16 * MIB + 24 * rows * window),
        cost_estimate=COST,
        name="attend",
    )(place, *partials, *fixed)


def on_device(groups, zs, ys, tokens, gain, w_query, w_kv, lengths, overlong, assign):
    count = tokens.shape[0]
    pair = 2 * count
    x, z, y, side = (lax.axis_index(name) for name in ("groups", "z", "y", "dp"))
    blk = z * ys + y
    width = w_query.shape[0] // groups
    peers = [(dx, dy) for dx in range(groups) for dy in range(ys)]
    pair_base = blk * pair
    block_base = pair_base // BLOCK
    slots = lax.dynamic_slice_in_dim(assign, block_base, 2) - block_base
    own_slot = lax.dynamic_index_in_dim(slots, side, keepdims=False)
    other_slot = lax.dynamic_index_in_dim(slots, 1 - side, keepdims=False)
    tokens_all = zs * ys * pair
    window = min(tokens_all // 2 + pair, tokens_all)
    first_key = jnp.maximum(pair_base - tokens_all // 2, 0)
    key_blk = first_key // pair + jnp.arange(window // pair, dtype=jnp.int32)
    spot = (blk % ys + ys - key_blk % ys) % ys + (z + zs - key_blk // ys) % zs * ys
    place = jnp.concatenate(
        [jnp.stack([side, own_slot, other_slot, first_key]).astype(jnp.int32), spot * pair]
    )

    own = jnp.concatenate(
        [
            lax.dynamic_slice_in_dim(w_kv, x * width, width, 0),
            lax.dynamic_slice_in_dim(w_query, x * width, width, 0),
        ],
        axis=1,
    )
    normed = norm_pieces(tokens, gain, zs, ys, groups, width)
    pair_rows = pair_base + jnp.arange(pair, dtype=jnp.int32)
    which, offset, masked = rollout_info(pair_rows, lengths, overlong)
    cosine, sine = rotation(offset)
    query_info = jnp.stack([which, pair_rows, masked], axis=1)
    key_place = first_key + jnp.arange(window, dtype=jnp.int32)
    ends = jnp.cumsum(lengths)
    which_key = jnp.sum((ends[:, None] <= key_place[None, :]).astype(jnp.int32), axis=0)[None, :]
    tables = (cosine, sine, query_info, which_key, place)

    near, *far = normed
    near = lax.all_to_all(near, ("groups", "y"), 0, 0, tiled=True)
    pieces = {("own", 0): own}
    if zs == 4:
        ends, middle = [(0, 1), (1, 0), (2, 3), (3, 2)], [(1, 2), (2, 1)]
        first = [lax.ppermute(own, "z", ends), lax.ppermute(own, "z", middle)]
        came = [lax.ppermute(first[0], "z", middle), lax.ppermute(first[1], "z", [(1, 0), (2, 3)])]
        pieces.update({("pair", 1 + at): block for at, block in enumerate(first + came)})
    else:
        came = [own, own]
        for step in range(1, zs - 1):
            came = [hop_down(came[0], step, zs), hop_up(came[1], step, zs)]
            pieces["down", step], pieces["up", step] = came
    far = lax.optimization_barrier((near, *far))[1:]
    far = [
        shift_square(part, dx, dy, groups, ys) if dx or dy else part
        for (dx, dy), part in zip(peers, far)
    ]
    mine = [near, jnp.stack(far)]
    done = (*mine, *came, *tables)
    others = [swap_core(mine[0]), swap_core(after(mine[1], *done))]
    came = [after(came[0], *done), after(came[1], *done)]
    cosine, sine, query_info, which_key, place = lax.optimization_barrier((*tables, near))[:5]
    cuts, first = [(0, HEAD)], HEAD
    for heads in CHUNK_HEADS:
        cuts.append((first, heads * HEAD))
        first += heads * HEAD
    parts = [cuts[0], (HEAD, own.shape[1] - HEAD)]
    last = []
    for a, n in parts:
        block = came[0][:, a : a + n]
        if zs != 4:
            block = jnp.where(z == 1, block, came[1][:, a : a + n])
        last.append(hop_ends(block, zs))
    sums = [collect(mine, others, pieces, [part], zs, ys, groups)[0] for part in parts]

    def to_owner(part, dx, dy):
        return shift_square(part, -dx, -dy, groups, ys) if dx or dy else part

    layout = [(0, HEAD, [at]) for at in range(len(peers))]
    kv_parts = finish(mine[1], others[1], last[0], sums[0], layout)
    proj = sum(to_owner(part[0], *peer) for part, peer in zip(kv_parts, peers))
    turned = proj * cosine + jnp.roll(proj, HEAD // 2, axis=1) * sine
    kept_kv = jnp.where(side == 0, turned, proj).astype(jnp.bfloat16)
    kept_kv, last[1] = lax.optimization_barrier((kept_kv, last[1]))
    beside = lax.ppermute(kept_kv, "y", [(i, (i + 1) % ys) for i in range(ys)])

    split = CHUNK_HEADS[0] * HEAD
    rest = CHUNK_HEADS[1] * HEAD
    layout = [(0, split, [dx * ys + dy for dy in range(ys)]) for dx in range(groups)]
    layout += [(split, rest, [dx * ys + dy for dx in range(groups)]) for dy in range(ys)]
    parts = finish(mine[1], others[1], last[1], sums[1], layout)
    beside, *parts = lax.optimization_barrier((beside, *parts))
    by_group = sum(to_owner(part, dx, 0) for dx, part in enumerate(parts[:groups]))
    by_y = sum(to_owner(part, 0, dy) for dy, part in enumerate(parts[groups:]))
    partials = [
        [to_owner(by_group[dy], 0, dy) for dy in range(ys)],
        [to_owner(by_y[dx], dx, 0) for dx in range(groups)],
    ]

    both = jnp.concatenate([kept_kv, beside], axis=0)
    along = [both] + [
        lax.ppermute(both, "z", [(i, (i + n) % zs) for i in range(zs)]) for n in range(1, zs)
    ]
    here = jnp.concatenate(along, axis=0)
    there = swap_core(here)

    kept, got = [], []
    for part in partials:
        owned, other = attend(part, cosine, sine, query_info, which_key, here, there, place)
        kept.append(owned)
        got.append(swap_core(other))
    kept = jnp.concatenate(kept, axis=1)
    got = jnp.concatenate(got, axis=1)
    return jnp.where(
        side == 0,
        jnp.concatenate([kept, got], axis=1),
        jnp.concatenate([got, kept], axis=1),
    )


def solution(mesh):
    groups, blks, cores = (mesh.shape[name] for name in ("groups", "blk", "dp"))
    ys = 2
    zs = blks // ys
    fine = Mesh(mesh.devices.reshape(groups, zs, ys, cores), ("groups", "z", "y", "dp"))
    placed = (
        P(("groups", "z", "y", "dp"), None),
        P(),
        P(("z", "y"), "dp"),
        P(("z", "y"), "dp"),
        P("groups"),
        P("groups"),
        P("groups"),
    )
    return jax.shard_map(
        functools.partial(on_device, groups, zs, ys),
        mesh=fine,
        in_specs=placed,
        out_specs=P(("groups", "z", "y", "dp"), None),
        check_vma=False,
    )
```
